32 devices in a mesh: days: 2 (over x), tm: 8 (over z, y), sta: 2 (over core).
Axes of the slice: x: 2, y: 2, z: 4, core: 2. Of those that a mesh axis runs over, the one named last changes fastest.
Arguments:
- records: bfloat16 [2048, 2048], P('sta', ('days', 'tm')), parts along dimension 1, may hold values from -6 to 6
- following: bfloat16 [2048, 510], P('sta', 'days'), parts along dimension 1, may hold values from -6 to 6
- library: bfloat16 [32, 2048, 256], P(None, ('sta', 'tm')), may hold values from -6 to 6
- template_ids: int32 [2, 8], replicated, may hold values from 0 to 31
- channel_mask: int32 [32, 2048], replicated, may hold values 0 or 1
- station_group: int32 [2048], replicated, may hold values from 0 to 127
Outputs:
- detection: float32 [2, 8, 2048], P('sta', None, ('days', 'tm')), parts along dimension 2
The draws below stay inside these ranges and needn't reach their ends.
There are 2 independent parts, one for each index of `days`. The reference program is written for one: setup_inputs(seed, part) draws one part's arguments, and reference() takes and returns one part's arrays. A program takes and returns all parts, laid end to end along the dimension named above; an argument that names none is the same for every part. Nothing has to cross between parts.
All inputs are finite; a program needn't handle non-finite values.
Results may differ from the reference program's by a relative error of at most 0.0003.
Values may be sent and summed in bfloat16 or wider, within the bound.
No kernel may reach another device: no remote copies, remote signals or barrier semaphores. Data moves between devices by JAX's collectives and lax.ppermute only.
A program may use at most 128 MiB of HBM per device.

```python
import math
import jax
import jax.numpy as jnp
import numpy as np
from jax import lax

S = 2048
W = 256
NLIB = 32
NB = 2
KB = 8
G = 128
T_SIZE = 1024


def touch_ends(values, key, low, largest):
    longest = values.shape.index(max(values.shape))
    spots = []
    for shift in (0, 1):
        where = [jax.random.randint(jax.random.fold_in(key, axis), (), 0, length) for axis, length in enumerate(values.shape)]
        where[longest] = (where[longest] + shift) % values.shape[longest]
        spots.append(tuple(where))
    return values.at[spots[0]].set(low).at[spots[1]].set(largest)


def shard_levels(own_key, shape, pieces, least, largest):
    gain, own = 1.0, jax.random.fold_in(own_key, 6)
    for axis_at, blocks in pieces:
        steps = jnp.exp(jax.random.uniform(jax.random.fold_in(own, axis_at), (blocks,), jnp.float32, least / len(pieces), largest / len(pieces)))
        gain = gain * jnp.repeat(steps, shape[axis_at] // blocks).reshape([-1 if axis == axis_at else 1 for axis in range(len(shape))])
    return gain


def rank_bounds(number_of, skew):
    portions = [(1 << 20) // math.isqrt(grade ** skew) + 1 for grade in range(1, number_of + 1)]
    spread = 1 + sum(portions) // (1 << 30)
    return np.cumsum(np.array([max(1, weight // spread) for weight in portions]))


def skewed_ids(own_key, extent, number_of, lean):
    table = rank_bounds(number_of, lean)
    lot = jax.random.randint(jax.random.fold_in(own_key, 1), extent, 0, int(table[number_of - 1]))
    standing = jnp.searchsorted(jnp.asarray(table, jnp.int32), lot, side="right")
    return jax.random.permutation(jax.random.fold_in(own_key, 2), number_of)[standing].astype(jnp.int32)


def scatter_about(key, extent, spread, reach, split=(), kind=jnp.bfloat16):
    array = spread * jax.random.normal(key, extent, jnp.float32)
    if split:
        array = array * shard_levels(key, extent, split, -0.22, 0.18)
    return jnp.clip(array, -reach, reach).astype(kind)


def setup_inputs(seed: int = 0, part: int = 0) -> dict:
    key_of = jax.random.split(jax.random.key(seed), 7)
    part_splits = jax.random.split(jax.random.fold_in(key_of[6], part), 7)
    return {
        "records": scatter_about(part_splits[0], (S, T_SIZE), 1.0, 6.0, ((0, 2), (1, 8))),
        "following": scatter_about(part_splits[1], (S, W - 1), 1.0, 6.0, ((0, 2),)),
        "library": scatter_about(key_of[2], (NLIB, S, W), 1.0, 6.0, ((1, 16),)),
        "template_ids": touch_ends(jax.random.randint(key_of[3], (NB, KB), 0, NLIB), jax.random.fold_in(key_of[3], 1), 0, NLIB - 1).astype(jnp.int32),
        "channel_mask": touch_ends((jax.random.randint(key_of[4], (NLIB, S), 0, 2) < 1).astype(jnp.int32), jax.random.fold_in(key_of[4], 1), 0, 1),
        "station_group": touch_ends(skewed_ids(key_of[5], (S,), G, 2), jax.random.fold_in(key_of[5], 3), 0, G - 1).astype(jnp.int32),
    }


epsilon = 1e-06

def reference(records, following, library, template_ids, channel_mask, station_group):
    stream = jnp.concatenate([records, following], axis=1)
    squares = stream.astype(jnp.float32) ** 2
    energy = lax.reduce_window(squares, jnp.float32(0), lax.add, (1, W), (1, 1), 'VALID') / W
    inverse = 1.0 / jnp.sqrt(energy + epsilon)
    onehot = (station_group[:, None] == jnp.arange(G, dtype=jnp.int32)[None, :]).astype(jnp.int32)
    counts = jnp.dot(channel_mask, onehot, preferred_element_type=jnp.int32)
    per_station = jnp.take(counts, station_group, axis=1)
    tmean = lax.optimization_barrier(jnp.mean(library.astype(jnp.float32) ** 2, axis=2))
    coef = channel_mask.astype(jnp.float32) / jnp.sqrt(jnp.float32(W * G) * jnp.maximum(per_station, 1).astype(jnp.float32) * (tmean + epsilon))
    flat_ids = template_ids.reshape(-1)
    chosen = jnp.take(library, flat_ids, axis=0)
    weights = jnp.take(coef, flat_ids, axis=0)
    block_size = math.gcd(S, 16)
    grid = jnp.arange(W, dtype=jnp.int32)[:, None] + jnp.arange(T_SIZE, dtype=jnp.int32)[None, :]

    def advance(running, index):
        first = (index * block_size).astype(jnp.int32)
        rows = lax.dynamic_slice_in_dim(stream, first, block_size, 0)
        hankel = rows[:, grid].astype(jnp.float32)
        temps = lax.dynamic_slice_in_dim(chosen, first, block_size, 1).astype(jnp.float32)
        corr = jnp.einsum('jbw,bwt->jbt', temps, hankel)
        weight = lax.dynamic_slice_in_dim(weights, first, block_size, 1)
        scale = lax.dynamic_slice_in_dim(inverse, first, block_size, 0)
        return (running + lax.optimization_barrier(jnp.sum(corr * weight[:, :, None] * scale[None], axis=1)), None)
    start_zero = jnp.zeros((NB * KB, T_SIZE), jnp.float32)
    result = lax.scan(advance, start_zero, jnp.arange(S // block_size, dtype=jnp.int32))[0]
    return result.reshape(NB, KB, T_SIZE)
```

```python
import functools

import jax
import jax.numpy as jnp
from jax import lax
from jax.experimental import pallas as pl
from jax.experimental.pallas import tpu as pltpu
from jax.sharding import PartitionSpec as P

W = 256
NB = 2
KB = 8
G = 128
SLOTS = NB * KB
PH = 8
LANES = 128
TAPS = W // PH
VMEM = 56 << 20

epsilon = 1e-06


def lane_ids(shape):
    return lax.broadcasted_iota(jnp.int32, shape, len(shape) - 1)


def shifted(here, after, by):
    if by == 0:
        return here
    lane = lane_ids(here.shape)
    return pltpu.roll(jnp.where(lane < by, after, here), LANES - by, here.ndim - 1)


def prepare_kernel(chunk, ids, library, mask, group, shifts, coef, picked, wide, rows, made, in_sem, out_sem):
    stations = library.shape[1]
    total = mask.shape[1]
    for k in range(SLOTS):
        pltpu.make_async_copy(library.at[ids[k // KB, k % KB]], picked.at[k], in_sem).start()

    for k in range(SLOTS):
        rows[pl.ds(k, 1), :] = mask[pl.ds(ids[k // KB, k % KB], 1), :].astype(jnp.float32)
    members = lax.broadcasted_iota(jnp.int32, (G, total), 0) == group[...]
    counts = lax.dot_general(
        rows[...].astype(jnp.bfloat16),
        members.astype(jnp.float32).astype(jnp.bfloat16),
        (((1,), (1,)), ((), ())),
        preferred_element_type=jnp.float32,
    )
    first = lax.axis_index("sta") * (stations * lax.axis_size("tm")) + lax.axis_index("tm") * stations
    block = pl.multiple_of(first // LANES * LANES, LANES)
    own_group = jnp.broadcast_to(group[:, pl.ds(block, LANES)], (G, LANES))
    own_mask = rows[:, pl.ds(block, LANES)]
    own = (lax.broadcasted_iota(jnp.int32, (G, LANES), 0) == own_group).astype(jnp.float32)
    per_station = jnp.dot(counts, own, preferred_element_type=jnp.float32, precision=lax.Precision.HIGHEST)
    scaled = own_mask / jnp.sqrt(jnp.float32(W * G) * jnp.maximum(per_station, 1.0))
    if stations % LANES:
        scaled = pltpu.roll(scaled, LANES - (first - block), 1)
    scaled = jnp.concatenate([scaled, jnp.zeros((LANES - SLOTS, LANES), jnp.float32)], axis=0).T

    for k in range(SLOTS):
        pltpu.make_async_copy(library.at[0], picked.at[k], in_sem).wait()
    for k in range(SLOTS):
        values = picked[k].astype(jnp.float32)
        wide[k] = values
        tmean = jnp.sum(values * values, axis=1, keepdims=True) / W
        value = scaled[:stations, k : k + 1] / jnp.sqrt(tmean + epsilon)
        coef[pl.ds(k * stations, stations), :] = jnp.broadcast_to(value, (stations, LANES))

    lane = lane_ids((PH, LANES))
    row = lax.broadcasted_iota(jnp.int32, (PH, LANES), 0)
    inside = lane >= row

    def station(s):
        for pair in range(SLOTS // 2):
            halves = []
            for k in (2 * pair, 2 * pair + 1):
                template = wide[k, pl.ds(s, 1), :]
                turned = [
                    pltpu.roll(
                        jnp.broadcast_to(template[:, h * LANES : (h + 1) * LANES], (PH, LANES)), 0, 1, stride=1, stride_axis=0
                    )
                    for h in range(W // LANES)
                ]
                halves.append(
                    jnp.concatenate(
                        [jnp.where(inside, turned[h], turned[h - 1]) for h in range(W // LANES)], axis=1
                    )
                )
            made[s, 2 * PH * pair : 2 * PH * (pair + 1), :] = jnp.concatenate(halves, axis=0).astype(jnp.bfloat16)

    def part(c, carry):
        def step(i, inner):
            station(c * chunk + i)
            return inner

        lax.fori_loop(0, chunk, step, 0, unroll=4)
        span = pl.ds(c * chunk, chunk)
        pltpu.make_async_copy(made.at[span], shifts.at[span], out_sem).start()
        return carry

    lax.fori_loop(0, stations // chunk, part, 0)
    pltpu.make_async_copy(made, shifts, out_sem).wait()


def prepare(template_ids, library, channel_mask, station_group):
    stations = library.shape[1]
    total = channel_mask.shape[1]
    chunk = min(16, stations)
    return pl.pallas_call(
        functools.partial(prepare_kernel, chunk),
        out_shape=(
            jax.ShapeDtypeStruct((stations, SLOTS * PH, W), jnp.bfloat16),
            jax.ShapeDtypeStruct((SLOTS * stations, LANES), jnp.float32),
        ),
        in_specs=[
            pl.BlockSpec(memory_space=pltpu.SMEM),
            pl.BlockSpec(memory_space=pl.ANY),
            pl.BlockSpec(memory_space=pltpu.VMEM),
            pl.BlockSpec(memory_space=pltpu.VMEM),
        ],
        out_specs=(pl.BlockSpec(memory_space=pl.ANY), pl.BlockSpec(memory_space=pltpu.VMEM)),
        scratch_shapes=[
            pltpu.VMEM((SLOTS, stations, W), jnp.bfloat16),
            pltpu.VMEM((SLOTS, stations, W), jnp.float32),
            pltpu.VMEM((SLOTS, total), jnp.float32),
            pltpu.VMEM((stations, SLOTS * PH, W), jnp.bfloat16),
            pltpu.SemaphoreType.DMA,
            pltpu.SemaphoreType.DMA,
        ],
        compiler_params=pltpu.CompilerParams(vmem_limit_bytes=VMEM),
        cost_estimate=pl.CostEstimate(flops=10_000_000, bytes_accessed=20_000_000, transcendentals=0),
        name="prepare",
    )(template_ids, library, channel_mask, station_group.reshape(1, total))


def correlate_kernel(unroll, chunk, moved, following, shifts, coef, out, held, tail, phases, inverse, sums, sems, tail_sem):
    owners, stations, block_len = moved.shape
    width = block_len // PH
    tiles = owners * block_len // (LANES * PH)
    per_tile = LANES // width
    position = lax.axis_index("tm")

    tail_copy = pltpu.make_async_copy(following.at[pl.ds(position * stations, stations)], tail, tail_sem)
    tail_copy.start()
    loads = [
        pltpu.make_async_copy(shifts.at[pl.ds(c * chunk, chunk)], held.at[pl.ds(c * chunk, chunk)], sems.at[c])
        for c in range(stations // chunk)
    ]
    for load in loads:
        load.start()

    time = lax.broadcasted_iota(jnp.int32, (W, W), 0)
    place = lax.broadcasted_iota(jnp.int32, (W, W), 1)
    order = (time == place % TAPS * PH + place // TAPS).astype(jnp.float32).astype(jnp.bfloat16)
    lane = lane_ids((stations, LANES))
    pieces = LANES // TAPS
    each = W // block_len
    for j in range(tiles):
        split = [
            jnp.dot(
                jnp.concatenate([moved[(j * pieces + q) * each + e] for e in range(each)], axis=1),
                order,
                preferred_element_type=jnp.float32,
            )
            for q in range(pieces)
        ]
        for p in range(PH):
            half, at = p // pieces, p % pieces
            value = None
            for q in range(pieces):
                piece = split[q][:, half * LANES : (half + 1) * LANES]
                if q != at:
                    piece = pltpu.roll(piece, (TAPS * (q - at)) % LANES, 1)
                value = piece if value is None else jnp.where(lane >= TAPS * q, piece, value)
            phases[j, pl.ds(p * stations, stations), :] = value
    tail_copy.wait()
    last = jnp.concatenate([tail[...], jnp.zeros((stations, 1), jnp.bfloat16)], axis=1)
    split = jnp.dot(last, order, preferred_element_type=jnp.float32)
    for p in range(PH):
        half, at = p // pieces, p % pieces
        piece = split[:, half * LANES : (half + 1) * LANES]
        phases[tiles, pl.ds(p * stations, stations), :] = pltpu.roll(piece, (-TAPS * at) % LANES, 1) if at else piece

    def norms(g, carry):
        windows = []
        for p in range(PH):
            at = pl.ds(p * stations + g * 8, 8)
            values = [jnp.square(phases[j, at, :]) for j in range(tiles + 1)]
            by = 1
            while by < TAPS:
                values = [v + shifted(v, values[min(j + 1, tiles)], by) for j, v in enumerate(values)]
                by *= 2
            windows.append(values)
        for j in range(tiles):
            later = [None] * (PH + 1)
            for p in reversed(range(PH)):
                later[p] = windows[p][j] if later[p + 1] is None else windows[p][j] + later[p + 1]
            before = None
            for p in range(PH):
                energy = later[p] if before is None else later[p] + before
                inverse[j, pl.ds(p * stations + g * 8, 8), :] = lax.rsqrt(energy / W + epsilon)
                following_one = shifted(windows[p][j], windows[p][j + 1], 1)
                before = following_one if before is None else before + following_one
        return carry

    lax.fori_loop(0, stations // 8, norms, 0, unroll=2)

    row = lax.broadcasted_iota(jnp.int32, (SLOTS * PH, LANES), 0) % PH
    inside = lane_ids((SLOTS * PH, LANES)) >= row
    nothing = jnp.zeros((SLOTS * PH, LANES), jnp.bfloat16)

    def station(s, totals):
        templates = held[s]
        head = templates[:, :LANES]
        main = jnp.concatenate([jnp.where(inside, head, nothing), templates[:, LANES:]], axis=1)
        rest = jnp.where(inside, nothing, head)[:, : 2 * PH]
        gains = coef[pl.ds(s, SLOTS, stride=stations), :]
        own = [phases[j, pl.ds(s, PH, stride=stations), :] for j in range(tiles + 1)]
        results = []
        for j in range(tiles):
            window = [shifted(own[j], own[j + 1], by) for by in range(TAPS + 1)]
            window.append(jnp.zeros_like(own[j]))
            pairs = [
                jnp.concatenate(window[2 * i : 2 * i + 2], axis=0).astype(jnp.bfloat16) for i in range(TAPS // 2 + 1)
            ]
            corr = jnp.dot(main, jnp.concatenate(pairs[:-1], axis=0), preferred_element_type=jnp.float32)
            corr = corr + jnp.dot(rest, pairs[-1], preferred_element_type=jnp.float32)
            scale = inverse[j, pl.ds(s, PH, stride=stations), :]
            results.append(
                totals[j] + (corr.reshape(SLOTS, PH, LANES) * scale[None]) * gains[:, None, :]
            )
        return tuple(results)

    totals = tuple(jnp.zeros((SLOTS, PH, LANES), jnp.float32) for _ in range(tiles))
    for c, load in enumerate(loads):
        load.wait()
        totals = lax.fori_loop(c * chunk, (c + 1) * chunk, station, totals, unroll=unroll)

    lane = lane_ids((PH, LANES))
    for d in range(owners):
        j, at = d // per_tile, d % per_tile
        for b in range(NB):
            value = None
            for k in range(KB):
                piece = totals[j][b * KB + k]
                if k != at:
                    piece = pltpu.roll(piece, (width * (k - at)) % LANES, 1)
                value = piece if value is None else jnp.where(lane >= width * k, piece, value)
            out[d, b] = value


def correlate(moved, following, shifts, coef):
    owners, stations, block_len = moved.shape
    tiles = owners * block_len // (LANES * PH)
    chunk = min(32, stations)
    return pl.pallas_call(
        functools.partial(correlate_kernel, 16, chunk),
        out_shape=jax.ShapeDtypeStruct((owners, NB, PH, LANES), jnp.float32),
        in_specs=[
            pl.BlockSpec(memory_space=pltpu.VMEM),
            pl.BlockSpec(memory_space=pl.ANY),
            pl.BlockSpec(memory_space=pl.ANY),
            pl.BlockSpec(memory_space=pltpu.VMEM),
        ],
        out_specs=pl.BlockSpec(memory_space=pltpu.VMEM),
        scratch_shapes=[
            pltpu.VMEM(shifts.shape, jnp.bfloat16),
            pltpu.VMEM((stations, following.shape[1]), jnp.bfloat16),
            pltpu.VMEM((tiles + 1, PH * stations, LANES), jnp.float32),
            pltpu.VMEM((tiles, PH * stations, LANES), jnp.float32),
            pltpu.VMEM((8, LANES), jnp.float32),
            pltpu.SemaphoreType.DMA((stations // chunk,)),
            pltpu.SemaphoreType.DMA,
        ],
        compiler_params=pltpu.CompilerParams(vmem_limit_bytes=VMEM),
        cost_estimate=pl.CostEstimate(flops=1_200_000_000, bytes_accessed=10_000_000, transcendentals=0),
        name="correlate",
    )(moved, following, shifts, coef)


def finish_kernel(parts, out):
    total = jnp.sum(parts[...], axis=0)
    width = LANES // KB
    lane = lane_ids((KB, LANES))
    source = lax.broadcasted_iota(jnp.int32, (KB, LANES), 0) * width + lane // PH
    value = None
    for p in range(PH):
        spread = jnp.take_along_axis(jnp.broadcast_to(total[p : p + 1, :], (KB, LANES)), source, axis=1)
        value = spread if value is None else jnp.where(lane % PH == p, spread, value)
    out[0] = value


def finish(parts):
    return pl.pallas_call(
        finish_kernel,
        out_shape=jax.ShapeDtypeStruct((1, KB, LANES), jnp.float32),
        in_specs=[pl.BlockSpec(memory_space=pltpu.VMEM)],
        out_specs=pl.BlockSpec(memory_space=pltpu.VMEM),
        name="finish",
    )(parts)


def shards(records, following, library, template_ids, channel_mask, station_group):
    owners = lax.axis_size("tm")
    block_len = records.shape[1]
    stations = library.shape[1]
    moved = lax.all_to_all(records.reshape(owners, stations, block_len), "tm", split_axis=0, concat_axis=0)
    shifts, coef = prepare(template_ids, library, channel_mask, station_group)
    partial_sum = correlate(moved, following, shifts, coef)
    parts = lax.all_to_all(
        partial_sum.reshape(owners * NB, PH, LANES), ("tm", "sta"), split_axis=0, concat_axis=0
    )
    return finish(parts)


def solution(mesh):
    placed = (
        P("sta", ("days", "tm")),
        P("sta", "days"),
        P(None, ("sta", "tm"), None),
        P(),
        P(),
        P(),
    )
    return jax.shard_map(
        shards,
        mesh=mesh,
        in_specs=placed,
        out_specs=P("sta", None, ("days", "tm")),
        check_vma=False,
    )
```

```python
import functools

import jax
import jax.numpy as jnp
from jax import lax
from jax.experimental import pallas as pl
from jax.experimental.pallas import tpu as pltpu
from jax.sharding import PartitionSpec as P

W = 256
NB = 2
KB = 8
G = 128
SLOTS = NB * KB
PH = 8
LANES = 128
TAPS = W // PH
VMEM = 24 << 20

epsilon = 1e-06


def lane_ids(shape):
    return lax.broadcasted_iota(jnp.int32, shape, len(shape) - 1)


def shifted(here, after, by):
    if by == 0:
        return here
    lane = lane_ids(here.shape)
    return pltpu.roll(jnp.where(lane < by, after, here), LANES - by, here.ndim - 1)


def prepare_kernel(ids, library, mask, group, made, coef, picked, wide, rows, in_sem):
    stations = library.shape[1]
    total = mask.shape[1]
    for k in range(SLOTS):
        pltpu.make_async_copy(library.at[ids[k // KB, k % KB]], picked.at[k], in_sem).start()

    for k in range(SLOTS):
        rows[pl.ds(k, 1), :] = mask[pl.ds(ids[k // KB, k % KB], 1), :].astype(jnp.float32)
    members = lax.broadcasted_iota(jnp.int32, (G, total), 0) == group[...]
    counts = lax.dot_general(
        rows[...].astype(jnp.bfloat16),
        members.astype(jnp.float32).astype(jnp.bfloat16),
        (((1,), (1,)), ((), ())),
        preferred_element_type=jnp.float32,
    )
    first = lax.axis_index("sta") * (stations * lax.axis_size("tm")) + lax.axis_index("tm") * stations
    block = pl.multiple_of(first // LANES * LANES, LANES)
    own_group = jnp.broadcast_to(group[:, pl.ds(block, LANES)], (G, LANES))
    own_mask = rows[:, pl.ds(block, LANES)]
    own = (lax.broadcasted_iota(jnp.int32, (G, LANES), 0) == own_group).astype(jnp.float32)
    per_station = jnp.dot(counts, own, preferred_element_type=jnp.float32, precision=lax.Precision.HIGHEST)
    scaled = own_mask / jnp.sqrt(jnp.float32(W * G) * jnp.maximum(per_station, 1.0))
    if stations % LANES:
        scaled = pltpu.roll(scaled, LANES - (first - block), 1)
    scaled = jnp.concatenate([scaled, jnp.zeros((LANES - SLOTS, LANES), jnp.float32)], axis=0).T

    for k in range(SLOTS):
        pltpu.make_async_copy(library.at[0], picked.at[k], in_sem).wait()
    for k in range(SLOTS):
        values = picked[k].astype(jnp.float32)
        wide[k] = values
        tmean = jnp.sum(values * values, axis=1, keepdims=True) / W
        value = scaled[:stations, k : k + 1] / jnp.sqrt(tmean + epsilon)
        coef[pl.ds(k * stations, stations), :] = jnp.broadcast_to(value, (stations, LANES))

    lane = lane_ids((PH, LANES))
    row = lax.broadcasted_iota(jnp.int32, (PH, LANES), 0)
    inside = lane >= row

    def station(s):
        for pair in range(SLOTS // 2):
            halves = []
            for k in (2 * pair, 2 * pair + 1):
                template = wide[k, pl.ds(s, 1), :]
                turned = [
                    pltpu.roll(
                        jnp.broadcast_to(template[:, h * LANES : (h + 1) * LANES], (PH, LANES)), 0, 1, stride=1, stride_axis=0
                    )
                    for h in range(W // LANES)
                ]
                halves.append(
                    jnp.concatenate(
                        [jnp.where(inside, turned[h], turned[h - 1]) for h in range(W // LANES)], axis=1
                    )
                )
            made[s, 2 * PH * pair : 2 * PH * (pair + 1), :] = jnp.concatenate(halves, axis=0).astype(jnp.bfloat16)

    def step(s, carry):
        station(s)
        return carry

    lax.fori_loop(0, stations, step, 0, unroll=4)


def prepare(template_ids, library, channel_mask, station_group):
    stations = library.shape[1]
    total = channel_mask.shape[1]
    return pl.pallas_call(
        prepare_kernel,
        out_shape=(
            pltpu.VMEM((stations, SLOTS * PH, W), jnp.bfloat16),
            pltpu.VMEM((SLOTS * stations, LANES), jnp.float32),
        ),
        in_specs=[
            pl.BlockSpec(memory_space=pltpu.SMEM),
            pl.BlockSpec(memory_space=pl.ANY),
            pl.BlockSpec(memory_space=pltpu.VMEM),
            pl.BlockSpec(memory_space=pltpu.VMEM),
        ],
        out_specs=(pl.BlockSpec(memory_space=pltpu.VMEM), pl.BlockSpec(memory_space=pltpu.VMEM)),
        scratch_shapes=[
            pltpu.VMEM((SLOTS, stations, W), jnp.bfloat16),
            pltpu.VMEM((SLOTS, stations, W), jnp.float32),
            pltpu.VMEM((SLOTS, total), jnp.float32),
            pltpu.SemaphoreType.DMA,
        ],
        compiler_params=pltpu.CompilerParams(vmem_limit_bytes=VMEM),
        cost_estimate=pl.CostEstimate(flops=10_000_000, bytes_accessed=20_000_000, transcendentals=0),
        name="prepare",
    )(template_ids, library, channel_mask, station_group.reshape(1, total))


def correlate_kernel(unroll, moved, following, held, coef, out, tail, phases, inverse, tail_sem):
    owners, stations, block_len = moved.shape
    width = block_len // PH
    tiles = owners * block_len // (LANES * PH)
    per_tile = LANES // width
    position = lax.axis_index("tm")

    tail_copy = pltpu.make_async_copy(following.at[pl.ds(position * stations, stations)], tail, tail_sem)
    tail_copy.start()

    time = lax.broadcasted_iota(jnp.int32, (W, W), 0)
    place = lax.broadcasted_iota(jnp.int32, (W, W), 1)
    order = (time == place % TAPS * PH + place // TAPS).astype(jnp.float32).astype(jnp.bfloat16)
    lane = lane_ids((stations, LANES))
    pieces = LANES // TAPS
    each = W // block_len
    for j in range(tiles):
        split = [
            jnp.dot(
                jnp.concatenate([moved[(j * pieces + q) * each + e] for e in range(each)], axis=1),
                order,
                preferred_element_type=jnp.float32,
            )
            for q in range(pieces)
        ]
        for p in range(PH):
            half, at = p // pieces, p % pieces
            value = None
            for q in range(pieces):
                piece = split[q][:, half * LANES : (half + 1) * LANES]
                if q != at:
                    piece = pltpu.roll(piece, (TAPS * (q - at)) % LANES, 1)
                value = piece if value is None else jnp.where(lane >= TAPS * q, piece, value)
            phases[j, pl.ds(p * stations, stations), :] = value
    tail_copy.wait()
    last = jnp.concatenate([tail[...], jnp.zeros((stations, 1), jnp.bfloat16)], axis=1)
    split = jnp.dot(last, order, preferred_element_type=jnp.float32)
    for p in range(PH):
        half, at = p // pieces, p % pieces
        piece = split[:, half * LANES : (half + 1) * LANES]
        phases[tiles, pl.ds(p * stations, stations), :] = pltpu.roll(piece, (-TAPS * at) % LANES, 1) if at else piece

    def norms(g, carry):
        windows = []
        for p in range(PH):
            at = pl.ds(p * stations + g * 8, 8)
            values = [jnp.square(phases[j, at, :]) for j in range(tiles + 1)]
            by = 1
            while by < TAPS:
                values = [v + shifted(v, values[min(j + 1, tiles)], by) for j, v in enumerate(values)]
                by *= 2
            windows.append(values)
        for j in range(tiles):
            later = [None] * (PH + 1)
            for p in reversed(range(PH)):
                later[p] = windows[p][j] if later[p + 1] is None else windows[p][j] + later[p + 1]
            before = None
            for p in range(PH):
                energy = later[p] if before is None else later[p] + before
                inverse[j, pl.ds(p * stations + g * 8, 8), :] = lax.rsqrt(energy / W + epsilon)
                following_one = shifted(windows[p][j], windows[p][j + 1], 1)
                before = following_one if before is None else before + following_one
        return carry

    lax.fori_loop(0, stations // 8, norms, 0, unroll=2)

    row = lax.broadcasted_iota(jnp.int32, (SLOTS * PH, LANES), 0) % PH
    inside = lane_ids((SLOTS * PH, LANES)) >= row
    nothing = jnp.zeros((SLOTS * PH, LANES), jnp.bfloat16)

    def station(s, totals):
        templates = held[s]
        head = templates[:, :LANES]
        main = jnp.concatenate([jnp.where(inside, head, nothing), templates[:, LANES:]], axis=1)
        rest = jnp.where(inside, nothing, head)[:, : 2 * PH]
        gains = coef[pl.ds(s, SLOTS, stride=stations), :]
        own = [phases[j, pl.ds(s, PH, stride=stations), :] for j in range(tiles + 1)]
        results = []
        for j in range(tiles):
            window = [shifted(own[j], own[j + 1], by) for by in range(TAPS + 1)]
            window.append(jnp.zeros_like(own[j]))
            pairs = [
                jnp.concatenate(window[2 * i : 2 * i + 2], axis=0).astype(jnp.bfloat16) for i in range(TAPS // 2 + 1)
            ]
            corr = jnp.dot(main, jnp.concatenate(pairs[:-1], axis=0), preferred_element_type=jnp.float32)
            corr = corr + jnp.dot(rest, pairs[-1], preferred_element_type=jnp.float32)
            scale = inverse[j, pl.ds(s, PH, stride=stations), :]
            results.append(
                totals[j] + (corr.reshape(SLOTS, PH, LANES) * scale[None]) * gains[:, None, :]
            )
        return tuple(results)

    totals = tuple(jnp.zeros((SLOTS, PH, LANES), jnp.float32) for _ in range(tiles))
    totals = lax.fori_loop(0, stations, station, totals, unroll=unroll)

    lane = lane_ids((PH, LANES))
    for d in range(owners):
        j, at = d // per_tile, d % per_tile
        for b in range(NB):
            value = None
            for k in range(KB):
                piece = totals[j][b * KB + k]
                if k != at:
                    piece = pltpu.roll(piece, (width * (k - at)) % LANES, 1)
                value = piece if value is None else jnp.where(lane >= width * k, piece, value)
            out[d, b] = value


def correlate(moved, following, shifts, coef):
    owners, stations, block_len = moved.shape
    tiles = owners * block_len // (LANES * PH)
    return pl.pallas_call(
        functools.partial(correlate_kernel, 16),
        out_shape=jax.ShapeDtypeStruct((owners, NB, PH, LANES), jnp.float32),
        in_specs=[
            pl.BlockSpec(memory_space=pltpu.VMEM),
            pl.BlockSpec(memory_space=pl.ANY),
            pl.BlockSpec(memory_space=pltpu.VMEM),
            pl.BlockSpec(memory_space=pltpu.VMEM),
        ],
        out_specs=pl.BlockSpec(memory_space=pltpu.VMEM),
        scratch_shapes=[
            pltpu.VMEM((stations, following.shape[1]), jnp.bfloat16),
            pltpu.VMEM((tiles + 1, PH * stations, LANES), jnp.float32),
            pltpu.VMEM((tiles, PH * stations, LANES), jnp.float32),
            pltpu.SemaphoreType.DMA,
        ],
        compiler_params=pltpu.CompilerParams(vmem_limit_bytes=VMEM),
        cost_estimate=pl.CostEstimate(flops=1_200_000_000, bytes_accessed=10_000_000, transcendentals=0),
        name="correlate",
    )(moved, following, pltpu.with_memory_space_constraint(shifts, pltpu.VMEM), pltpu.with_memory_space_constraint(coef, pltpu.VMEM))


def finish_kernel(parts, out):
    total = jnp.sum(parts[...], axis=0)
    width = LANES // KB
    lane = lane_ids((KB, LANES))
    source = lax.broadcasted_iota(jnp.int32, (KB, LANES), 0) * width + lane // PH
    value = None
    for p in range(PH):
        spread = jnp.take_along_axis(jnp.broadcast_to(total[p : p + 1, :], (KB, LANES)), source, axis=1)
        value = spread if value is None else jnp.where(lane % PH == p, spread, value)
    out[0] = value


def finish(parts):
    return pl.pallas_call(
        finish_kernel,
        out_shape=jax.ShapeDtypeStruct((1, KB, LANES), jnp.float32),
        in_specs=[pl.BlockSpec(memory_space=pltpu.VMEM)],
        out_specs=pl.BlockSpec(memory_space=pltpu.VMEM),
        name="finish",
    )(parts)


def shards(records, following, library, template_ids, channel_mask, station_group):
    owners = lax.axis_size("tm")
    block_len = records.shape[1]
    stations = library.shape[1]
    moved = lax.all_to_all(records.reshape(owners, stations, block_len), "tm", split_axis=0, concat_axis=0)
    shifts, coef = prepare(template_ids, library, channel_mask, station_group)
    partial_sum = correlate(moved, following, shifts, coef)
    parts = lax.all_to_all(
        partial_sum.reshape(owners * NB, PH, LANES), ("tm", "sta"), split_axis=0, concat_axis=0
    )
    return finish(parts)


def solution(mesh):
    placed = (
        P("sta", ("days", "tm")),
        P("sta", "days"),
        P(None, ("sta", "tm"), None),
        P(),
        P(),
        P(),
    )
    return jax.shard_map(
        shards,
        mesh=mesh,
        in_specs=placed,
        out_specs=P("sta", None, ("days", "tm")),
        check_vma=False,
    )
```

```python
import functools
import math

import jax
import jax.numpy as jnp
from jax import lax
from jax.experimental import pallas as pl
from jax.experimental.pallas import tpu as pltpu
from jax.sharding import PartitionSpec as P

W = 256
NB = 2
KB = 8
G = 128
SLOTS = NB * KB
PH = 8
LANES = 128
TAPS = W // PH
PIECES = LANES // TAPS
VMEM = 24 << 20
CHUNK = 64

epsilon = 1e-06


def lane_ids(shape):
    return lax.broadcasted_iota(jnp.int32, shape, len(shape) - 1)


def shifted(here, after, by):
    if by == 0:
        return here
    lane = lane_ids(here.shape)
    return pltpu.roll(jnp.where(lane < by, after, here), LANES - by, here.ndim - 1)


def swap_groups(values, width):
    lane = lane_ids(values[0].shape)
    step = len(values) // 2
    while step:
        values = list(values)
        low = lane // (width * step) % 2 == 0
        for q in range(len(values)):
            if q // step % 2 == 0:
                a, b = values[q], values[q + step]
                values[q] = jnp.where(low, a, pltpu.roll(b, width * step, b.ndim - 1))
                values[q + step] = jnp.where(low, pltpu.roll(a, LANES - width * step, a.ndim - 1), b)
        step //= 2
    return values


def prepare_kernel(chunk, ids, library, mask, group, shifts, coef, picked, wide, rows, made, gains, row_sem, in_sem, out_sem, gain_sem):
    stations = library.shape[1]
    total = mask.shape[1]
    for k in range(SLOTS):
        pltpu.make_async_copy(mask.at[pl.ds(ids[k // KB, k % KB], 1)], rows.at[pl.ds(k, 1)], row_sem).start()
    for k in range(SLOTS):
        pltpu.make_async_copy(library.at[ids[k // KB, k % KB]], picked.at[k], in_sem).start()
    pltpu.make_async_copy(mask.at[pl.ds(0, SLOTS)], rows, row_sem).wait()

    members = lax.broadcasted_iota(jnp.int32, (G, total), 0) == group[...]
    counts = lax.dot_general(
        rows[...].astype(jnp.float32).astype(jnp.bfloat16),
        members.astype(jnp.float32).astype(jnp.bfloat16),
        (((1,), (1,)), ((), ())),
        preferred_element_type=jnp.float32,
    )
    first = lax.axis_index("sta") * (stations * lax.axis_size("tm")) + lax.axis_index("tm") * stations
    block = pl.multiple_of(first // LANES * LANES, LANES)
    own_group = jnp.broadcast_to(group[:, pl.ds(block, LANES)], (G, LANES))
    own_mask = rows[:, pl.ds(block, LANES)].astype(jnp.float32)
    own = (lax.broadcasted_iota(jnp.int32, (G, LANES), 0) == own_group).astype(jnp.float32)
    per_station = jnp.dot(counts, own, preferred_element_type=jnp.float32, precision=lax.Precision.HIGHEST)
    scaled = own_mask / jnp.sqrt(jnp.float32(W * G) * jnp.maximum(per_station, 1.0))
    if stations % LANES:
        scaled = pltpu.roll(scaled, LANES - (first - block), 1)
    scaled = jnp.concatenate([scaled, jnp.zeros((LANES - SLOTS, LANES), jnp.float32)], axis=0).T

    for k in range(SLOTS):
        pltpu.make_async_copy(library.at[0], picked.at[k], in_sem).wait()
    columns = []
    for k in range(SLOTS):
        values = picked[k].astype(jnp.float32)
        wide[k] = values
        tmean = jnp.sum(values * values, axis=1, keepdims=True) / W
        value = scaled[:stations, k : k + 1] / jnp.sqrt(tmean + epsilon)
        columns.append(jnp.broadcast_to(value, (stations, LANES)))
    gains[...] = jnp.swapaxes(jnp.stack(columns), 0, 1)
    gains_out = pltpu.make_async_copy(gains, coef, gain_sem)
    gains_out.start()

    lane = lane_ids((PH, LANES))
    row = lax.broadcasted_iota(jnp.int32, (PH, LANES), 0)
    inside = lane >= row

    def station(s):
        for pair in range(SLOTS // 2):
            halves = []
            for k in (2 * pair, 2 * pair + 1):
                template = wide[k, pl.ds(s, 1), :]
                turned = [
                    pltpu.roll(
                        jnp.broadcast_to(template[:, h * LANES : (h + 1) * LANES], (PH, LANES)), 0, 1, stride=1, stride_axis=0
                    )
                    for h in range(W // LANES)
                ]
                halves.append(
                    jnp.concatenate(
                        [jnp.where(inside, turned[h], turned[h - 1]) for h in range(W // LANES)], axis=1
                    )
                )
            made[s, 2 * PH * pair : 2 * PH * (pair + 1), :] = jnp.concatenate(halves, axis=0).astype(jnp.bfloat16)

    def part(c, carry):
        def step(i, inner):
            station(c * chunk + i)
            return inner

        lax.fori_loop(0, chunk, step, 0, unroll=True)
        span = pl.ds(c * chunk, chunk)
        pltpu.make_async_copy(made.at[span], shifts.at[span], out_sem).start()
        return carry

    lax.fori_loop(0, stations // chunk, part, 0)
    gains_out.wait()
    pltpu.make_async_copy(made, shifts, out_sem).wait()


def prepare(template_ids, library, channel_mask, station_group):
    stations = library.shape[1]
    total = channel_mask.shape[1]
    chunk = min(16, stations)
    return pl.pallas_call(
        functools.partial(prepare_kernel, chunk),
        out_shape=(
            pltpu.HBM((stations, SLOTS * PH, W), jnp.bfloat16),
            pltpu.HBM((stations, SLOTS, LANES), jnp.float32),
        ),
        in_specs=[
            pl.BlockSpec(memory_space=pltpu.SMEM),
            pl.BlockSpec(memory_space=pl.ANY),
            pl.BlockSpec(memory_space=pl.ANY),
            pl.BlockSpec(memory_space=pltpu.VMEM),
        ],
        out_specs=(pl.BlockSpec(memory_space=pl.ANY), pl.BlockSpec(memory_space=pl.ANY)),
        scratch_shapes=[
            pltpu.VMEM((SLOTS, stations, W), jnp.bfloat16),
            pltpu.VMEM((SLOTS, stations, W), jnp.float32),
            pltpu.VMEM((SLOTS, total), jnp.int32),
            pltpu.VMEM((stations, SLOTS * PH, W), jnp.bfloat16),
            pltpu.VMEM((stations, SLOTS, LANES), jnp.float32),
            pltpu.SemaphoreType.DMA,
            pltpu.SemaphoreType.DMA,
            pltpu.SemaphoreType.DMA,
            pltpu.SemaphoreType.DMA,
        ],
        compiler_params=pltpu.CompilerParams(vmem_limit_bytes=VMEM),
        cost_estimate=pl.CostEstimate(flops=10_000_000, bytes_accessed=20_000_000, transcendentals=0),
        name="prepare",
    )(
        template_ids,
        *(pltpu.with_memory_space_constraint(v, pltpu.HBM) for v in (library, channel_mask, station_group.reshape(1, total))),
    )


def correlate_kernel(chunk, moved, following, shifts, coef, out, held, gains, tail, phases, inverse, held_sems, gain_sem, tail_sem):
    owners, stations, block_len = moved.shape
    width = block_len // PH
    tiles = owners * block_len // (LANES * PH)
    per_tile = LANES // width
    position = lax.axis_index("tm")

    tail_copy = pltpu.make_async_copy(following.at[pl.ds(position * stations, stations)], tail, tail_sem)
    tail_copy.start()
    held_copies = [
        pltpu.make_async_copy(shifts.at[pl.ds(c, chunk)], held.at[pl.ds(c, chunk)], held_sems.at[c // chunk])
        for c in range(0, stations, chunk)
    ]
    held_copies[0].start()
    gain_copy = pltpu.make_async_copy(coef, gains, gain_sem)
    gain_copy.start()
    for copy in held_copies[1:]:
        copy.start()

    time = lax.broadcasted_iota(jnp.int32, (W, W), 0)
    place = lax.broadcasted_iota(jnp.int32, (W, W), 1)
    sample = place % TAPS * PH + place // TAPS
    order = (time == sample).astype(jnp.float32).astype(jnp.bfloat16)
    here = (time >= sample).astype(jnp.float32).astype(jnp.bfloat16)
    beyond = (time < sample).astype(jnp.float32).astype(jnp.bfloat16)

    def squares(rows):
        value = jnp.square(rows.astype(jnp.float32))
        high = value.astype(jnp.bfloat16)
        return high, (value - high.astype(jnp.float32)).astype(jnp.bfloat16)

    def spread(target, j, split):
        parts = []
        for half in range(PH // PIECES):
            parts += swap_groups([v[:, half * LANES : (half + 1) * LANES] for v in split], TAPS)
        target[j] = jnp.swapaxes(jnp.stack(parts), 0, 1)

    each = W // block_len
    rows = [
        jnp.concatenate([moved[q * each + e] for e in range(each)], axis=1) for q in range(tiles * PIECES)
    ]
    for j in range(tiles):
        spread(
            phases,
            j,
            [jnp.dot(rows[j * PIECES + q], order, preferred_element_type=jnp.float32) for q in range(PIECES)],
        )
    tail_copy.wait()
    rows.append(jnp.concatenate([tail[...], jnp.zeros((stations, 1), jnp.bfloat16)], axis=1))
    split = jnp.dot(rows[-1], order, preferred_element_type=jnp.float32)
    parts = []
    for p in range(PH):
        half, at = p // PIECES, p % PIECES
        piece = split[:, half * LANES : (half + 1) * LANES]
        parts.append(pltpu.roll(piece, (-TAPS * at) % LANES, 1) if at else piece)
    phases[tiles] = jnp.swapaxes(jnp.stack(parts), 0, 1)

    squared = [squares(r) for r in rows]
    for j in range(tiles):
        split = []
        for q in range(j * PIECES, (j + 1) * PIECES):
            energy = sum(
                jnp.dot(part, matrix, preferred_element_type=jnp.float32)
                for parts, matrix in ((squared[q], here), (squared[q + 1], beyond))
                for part in parts
            )
            split.append(lax.rsqrt(energy / W + epsilon))
        spread(inverse, j, split)

    row = lax.broadcasted_iota(jnp.int32, (2 * PH, LANES), 0) % PH
    inside = (lane_ids((2 * PH, LANES)) >= row).astype(jnp.float32).astype(jnp.bfloat16)

    def station(s, totals):
        templates = held[s]
        head = templates[:, :LANES].reshape(SLOTS // 2, 2 * PH, LANES)
        kept = head * inside[None]
        rest = (head - kept).reshape(SLOTS * PH, LANES)[:, : 2 * PH]
        main = jnp.concatenate([kept.reshape(SLOTS * PH, LANES), templates[:, LANES:], rest], axis=1)
        gain = gains[s]
        own = [phases[j, s] for j in range(tiles + 1)]
        results = []
        for j in range(tiles):
            window = [shifted(own[j], own[j + 1], by) for by in range(TAPS + 1)]
            window.append(jnp.zeros_like(own[j]))
            pairs = [
                jnp.concatenate(window[2 * i : 2 * i + 2], axis=0).astype(jnp.bfloat16) for i in range(TAPS // 2 + 1)
            ]
            corr = jnp.dot(main, jnp.concatenate(pairs, axis=0), preferred_element_type=jnp.float32)
            scale = inverse[j, s]
            results.append(totals[j] + (corr.reshape(SLOTS, PH, LANES) * scale[None]) * gain[:, None, :])
        return tuple(results)

    totals = tuple(jnp.zeros((SLOTS, PH, LANES), jnp.float32) for _ in range(tiles))
    gain_copy.wait()

    def part(c, totals):
        span = pl.ds(c * chunk, chunk)
        pltpu.make_async_copy(shifts.at[span], held.at[span], held_sems.at[c]).wait()
        return lax.fori_loop(0, chunk, lambda i, totals: station(c * chunk + i, totals), totals, unroll=True)

    totals = lax.fori_loop(0, stations // chunk, part, totals)

    lane = lane_ids((KB, LANES))
    source = lax.broadcasted_iota(jnp.int32, (KB, LANES), 0) * width + lane // PH
    for j in range(tiles):
        for b in range(NB):
            tile = swap_groups([totals[j][b * KB + k] for k in range(KB)], width)
            for at in range(per_tile):
                value = None
                for p in range(PH):
                    one = jnp.broadcast_to(tile[at][p : p + 1, :], (KB, LANES))
                    one = jnp.take_along_axis(one, source, axis=1)
                    value = one if value is None else jnp.where(lane % PH == p, one, value)
                out[j * per_tile + at, b] = value


def correlate(moved, following, shifts, coef):
    owners, stations, block_len = moved.shape
    tiles = owners * block_len // (LANES * PH)
    chunk = math.gcd(stations, CHUNK)
    return pl.pallas_call(
        functools.partial(correlate_kernel, chunk),
        out_shape=jax.ShapeDtypeStruct((owners, NB, KB, LANES), jnp.float32),
        in_specs=[
            pl.BlockSpec(memory_space=pltpu.VMEM),
            pl.BlockSpec(memory_space=pl.ANY),
            pl.BlockSpec(memory_space=pl.ANY),
            pl.BlockSpec(memory_space=pl.ANY),
        ],
        out_specs=pl.BlockSpec(memory_space=pltpu.VMEM),
        scratch_shapes=[
            pltpu.VMEM(shifts.shape, jnp.bfloat16),
            pltpu.VMEM(coef.shape, jnp.float32),
            pltpu.VMEM((stations, following.shape[1]), jnp.bfloat16),
            pltpu.VMEM((tiles + 1, stations, PH, LANES), jnp.float32),
            pltpu.VMEM((tiles, stations, PH, LANES), jnp.float32),
            pltpu.SemaphoreType.DMA((stations // chunk,)),
            pltpu.SemaphoreType.DMA,
            pltpu.SemaphoreType.DMA,
        ],
        compiler_params=pltpu.CompilerParams(vmem_limit_bytes=VMEM),
        cost_estimate=pl.CostEstimate(flops=1_200_000_000, bytes_accessed=10_000_000, transcendentals=0),
        name="correlate",
    )(moved, *(pltpu.with_memory_space_constraint(v, pltpu.HBM) for v in (following, shifts, coef)))


def shards(records, following, library, template_ids, channel_mask, station_group):
    owners = lax.axis_size("tm")
    block_len = records.shape[1]
    stations = library.shape[1]
    moved = lax.all_to_all(records.reshape(owners, stations, block_len), "tm", split_axis=0, concat_axis=0)
    shifts, coef = prepare(template_ids, library, channel_mask, station_group)
    partial_sum = correlate(moved, following, shifts, coef)
    parts = lax.all_to_all(
        partial_sum.reshape(owners * NB, KB, block_len), ("tm", "sta"), split_axis=0, concat_axis=0
    )
    return jnp.sum(parts, axis=0)[None]


def solution(mesh):
    placed = (
        P("sta", ("days", "tm")),
        P("sta", "days"),
        P(None, ("sta", "tm"), None),
        P(),
        P(),
        P(),
    )
    return jax.shard_map(
        shards,
        mesh=mesh,
        in_specs=placed,
        out_specs=P("sta", None, ("days", "tm")),
        check_vma=False,
    )
```

```python
import functools
import math

import jax
import jax.numpy as jnp
from jax import lax
from jax.experimental import pallas as pl
from jax.experimental.pallas import tpu as pltpu
from jax.sharding import PartitionSpec as P

W = 256
NB = 2
KB = 8
G = 128
SLOTS = NB * KB
PH = 8
LANES = 128
TAPS = W // PH
PIECES = LANES // TAPS
VMEM = 24 << 20
CHUNK = 64

epsilon = 1e-06


def lane_ids(shape):
    return lax.broadcasted_iota(jnp.int32, shape, len(shape) - 1)


def shifted(here, after, by):
    if by == 0:
        return here
    lane = lane_ids(here.shape)
    return pltpu.roll(jnp.where(lane < by, after, here), LANES - by, here.ndim - 1)


def swap_groups(values, width):
    lane = lane_ids(values[0].shape)
    step = len(values) // 2
    while step:
        values = list(values)
        low = lane // (width * step) % 2
        low = (low if values[0].dtype == jnp.float32 else low.astype(jnp.float32).astype(values[0].dtype)) == 0
        for q in range(len(values)):
            if q // step % 2 == 0:
                a, b = values[q], values[q + step]
                values[q] = jnp.where(low, a, pltpu.roll(b, width * step, b.ndim - 1))
                values[q + step] = jnp.where(low, pltpu.roll(a, LANES - width * step, a.ndim - 1), b)
        step //= 2
    return values


def prepare_kernel(
    chunk,
    ids,
    library,
    mask,
    group,
    following,
    shifts,
    coef,
    after,
    picked,
    wide,
    rows,
    made,
    gains,
    own_tail,
    tail,
    row_sem,
    in_sem,
    tail_sem,
    out_sem,
    gain_sem,
    after_sem,
):
    stations = library.shape[1]
    total = mask.shape[1]
    position = lax.axis_index("tm")
    for k in range(SLOTS):
        pltpu.make_async_copy(mask.at[pl.ds(ids[k // KB, k % KB], 1)], rows.at[pl.ds(k, 1)], row_sem).start()
    for k in range(SLOTS):
        pltpu.make_async_copy(library.at[ids[k // KB, k % KB]], picked.at[k], in_sem).start()
    tail_in = pltpu.make_async_copy(following.at[pl.ds(position * stations, stations)], own_tail, tail_sem)
    tail_in.start()

    members = lax.broadcasted_iota(jnp.int32, (G, total), 0) == group[...]
    members = members.astype(jnp.float32).astype(jnp.bfloat16)
    pltpu.make_async_copy(mask.at[pl.ds(0, SLOTS)], rows, row_sem).wait()
    counts = lax.dot_general(
        rows[...].astype(jnp.float32).astype(jnp.bfloat16),
        members,
        (((1,), (1,)), ((), ())),
        preferred_element_type=jnp.float32,
    )
    first = lax.axis_index("sta") * (stations * lax.axis_size("tm")) + position * stations
    block = pl.multiple_of(first // LANES * LANES, LANES)
    own_group = jnp.broadcast_to(group[:, pl.ds(block, LANES)], (G, LANES))
    own_mask = rows[:, pl.ds(block, LANES)].astype(jnp.float32)
    own = (lax.broadcasted_iota(jnp.int32, (G, LANES), 0) == own_group).astype(jnp.float32)
    per_station = jnp.dot(counts, own, preferred_element_type=jnp.float32, precision=lax.Precision.HIGHEST)
    scaled = own_mask / jnp.sqrt(jnp.float32(W * G) * jnp.maximum(per_station, 1.0))
    if stations % LANES:
        scaled = pltpu.roll(scaled, LANES - (first - block), 1)
    scaled = jnp.concatenate([scaled, jnp.zeros((LANES - SLOTS, LANES), jnp.float32)], axis=0).T

    for k in range(SLOTS):
        pltpu.make_async_copy(library.at[0], picked.at[k], in_sem).wait()
    columns = []
    for k in range(SLOTS):
        values = picked[k].astype(jnp.float32)
        wide[k] = values
        tmean = jnp.sum(values * values, axis=1, keepdims=True) / W
        value = scaled[:stations, k : k + 1] / jnp.sqrt(tmean + epsilon)
        columns.append(jnp.broadcast_to(value, (stations, LANES)))
    gains[...] = jnp.swapaxes(jnp.stack(columns), 0, 1)
    gains_out = pltpu.make_async_copy(gains, coef, gain_sem)
    gains_out.start()
    tail_in.wait()
    tail[...] = jnp.concatenate([own_tail[...], jnp.zeros((stations, 1), jnp.bfloat16)], axis=1)
    tail_out = pltpu.make_async_copy(tail, after, after_sem)
    tail_out.start()

    lane = lane_ids((PH, LANES))
    row = lax.broadcasted_iota(jnp.int32, (PH, LANES), 0)
    inside = lane >= row

    def station(s):
        for pair in range(SLOTS // 2):
            halves = []
            for k in (2 * pair, 2 * pair + 1):
                template = wide[k, pl.ds(s, 1), :]
                turned = [
                    pltpu.roll(
                        jnp.broadcast_to(template[:, h * LANES : (h + 1) * LANES], (PH, LANES)), 0, 1, stride=1, stride_axis=0
                    )
                    for h in range(W // LANES)
                ]
                halves.append(
                    jnp.concatenate(
                        [jnp.where(inside, turned[h], turned[h - 1]) for h in range(W // LANES)], axis=1
                    )
                )
            made[s, 2 * PH * pair : 2 * PH * (pair + 1), :] = jnp.concatenate(halves, axis=0).astype(jnp.bfloat16)

    def part(c, carry):
        def step(i, inner):
            station(c * chunk + i)
            return inner

        lax.fori_loop(0, chunk, step, 0, unroll=True)
        span = pl.ds(c * chunk, chunk)
        pltpu.make_async_copy(made.at[span], shifts.at[span], out_sem).start()
        return carry

    lax.fori_loop(0, stations // chunk, part, 0)
    gains_out.wait()
    tail_out.wait()
    pltpu.make_async_copy(made, shifts, out_sem).wait()


def prepare(template_ids, library, channel_mask, station_group, following):
    stations = library.shape[1]
    total = channel_mask.shape[1]
    chunk = min(16, stations)
    inputs = template_ids, library, channel_mask, station_group.reshape(1, total), following
    return pl.pallas_call(
        functools.partial(prepare_kernel, chunk),
        out_shape=(
            pltpu.HBM((stations, SLOTS * PH, W), jnp.bfloat16),
            pltpu.HBM((stations, SLOTS, LANES), jnp.float32),
            pltpu.HBM((stations, W), jnp.bfloat16),
        ),
        in_specs=[
            pl.BlockSpec(memory_space=pltpu.SMEM),
            pl.BlockSpec(memory_space=pl.ANY),
            pl.BlockSpec(memory_space=pl.ANY),
            pl.BlockSpec(memory_space=pltpu.VMEM),
            pl.BlockSpec(memory_space=pl.ANY),
        ],
        out_specs=[pl.BlockSpec(memory_space=pl.ANY)] * 3,
        scratch_shapes=[
            pltpu.VMEM((SLOTS, stations, W), jnp.bfloat16),
            pltpu.VMEM((SLOTS, stations, W), jnp.float32),
            pltpu.VMEM((SLOTS, total), jnp.int32),
            pltpu.VMEM((stations, SLOTS * PH, W), jnp.bfloat16),
            pltpu.VMEM((stations, SLOTS, LANES), jnp.float32),
            pltpu.VMEM((stations, following.shape[1]), jnp.bfloat16),
            pltpu.VMEM((stations, W), jnp.bfloat16),
        ]
        + [pltpu.SemaphoreType.DMA] * 6,
        compiler_params=pltpu.CompilerParams(vmem_limit_bytes=VMEM),
        cost_estimate=pl.CostEstimate(flops=10_000_000, bytes_accessed=20_000_000, transcendentals=0),
        name="prepare",
    )(*(pltpu.with_memory_space_constraint(v, pltpu.HBM) for v in inputs))


def correlate_kernel(chunk, moved, following, shifts, coef, out, held, gains, tail, phases, inverse, held_sems, gain_sem, tail_sem):
    owners, stations, block_len = moved.shape
    width = block_len // PH
    tiles = owners * block_len // (LANES * PH)
    per_tile = LANES // width

    tail_copy = pltpu.make_async_copy(following, tail, tail_sem)
    tail_copy.start()
    held_copies = [
        pltpu.make_async_copy(shifts.at[pl.ds(c, chunk)], held.at[pl.ds(c, chunk)], held_sems.at[c // chunk])
        for c in range(0, stations, chunk)
    ]
    held_copies[0].start()
    gain_copy = pltpu.make_async_copy(coef, gains, gain_sem)
    gain_copy.start()
    for copy in held_copies[1:]:
        copy.start()

    time = lax.broadcasted_iota(jnp.int32, (W, W), 0)
    place = lax.broadcasted_iota(jnp.int32, (W, W), 1)
    order = (time == place % TAPS * PH + place // TAPS).astype(jnp.float32).astype(jnp.bfloat16)

    def split(rows):
        value = jnp.dot(rows, order, preferred_element_type=jnp.float32).astype(jnp.bfloat16)
        return [value[:, h * LANES : (h + 1) * LANES] for h in range(W // LANES)]

    def keep(target, j, parts):
        parts = jnp.stack([v.astype(jnp.float32) for v in parts])
        target[j] = jnp.swapaxes(parts, 0, 1)

    here = (time >= place % TAPS * PH + place // TAPS).astype(jnp.float32).astype(jnp.bfloat16)
    beyond = (time < place % TAPS * PH + place // TAPS).astype(jnp.float32).astype(jnp.bfloat16)

    def squares(rows):
        value = jnp.square(rows.astype(jnp.float32))
        high = value.astype(jnp.bfloat16)
        return high, (value - high.astype(jnp.float32)).astype(jnp.bfloat16)

    each = W // block_len
    rows = [
        jnp.concatenate([moved[q * each + e] for e in range(each)], axis=1) for q in range(tiles * PIECES)
    ]
    for j in range(tiles):
        pieces = [split(r) for r in rows[j * PIECES : (j + 1) * PIECES]]
        keep(phases, j, [v for h in range(PH // PIECES) for v in swap_groups([p[h] for p in pieces], TAPS)])
    tail_copy.wait()
    rows.append(tail[...])
    last = split(rows[-1])
    keep(
        phases,
        tiles,
        [
            pltpu.roll(last[p // PIECES], LANES - TAPS * (p % PIECES), 1) if p % PIECES else last[p // PIECES]
            for p in range(PH)
        ],
    )

    squared = [squares(r) for r in rows]
    for j in range(tiles):
        pieces = []
        for q in range(j * PIECES, (j + 1) * PIECES):
            energy = sum(
                jnp.dot(part, matrix, preferred_element_type=jnp.float32)
                for parts, matrix in ((squared[q], here), (squared[q + 1], beyond))
                for part in parts
            )
            energy = lax.rsqrt(energy / W + epsilon)
            pieces.append([energy[:, h * LANES : (h + 1) * LANES] for h in range(W // LANES)])
        keep(inverse, j, [v for h in range(PH // PIECES) for v in swap_groups([p[h] for p in pieces], TAPS)])

    row = lax.broadcasted_iota(jnp.int32, (2 * PH, LANES), 0) % PH
    inside = (lane_ids((2 * PH, LANES)) >= row).astype(jnp.float32).astype(jnp.bfloat16)

    def station(s, totals):
        templates = held[s]
        head = templates[:, :LANES].reshape(SLOTS // 2, 2 * PH, LANES)
        kept = head * inside[None]
        rest = (head - kept).reshape(SLOTS * PH, LANES)[:, : 2 * PH]
        main = jnp.concatenate([kept.reshape(SLOTS * PH, LANES), templates[:, LANES:], rest], axis=1)
        gain = [jnp.broadcast_to(gains[s, pl.ds(k, 1), :], (PH, LANES)) for k in range(SLOTS)]
        own = [phases[j, s] for j in range(tiles + 1)]
        results = []
        for j in range(tiles):
            window = [shifted(own[j], own[j + 1], by) for by in range(TAPS + 1)]
            window.append(jnp.zeros_like(own[j]))
            pairs = [
                jnp.concatenate(window[2 * i : 2 * i + 2], axis=0).astype(jnp.bfloat16) for i in range(TAPS // 2 + 1)
            ]
            corr = jnp.dot(main, jnp.concatenate(pairs, axis=0), preferred_element_type=jnp.float32)
            scale = inverse[j, s]
            corr = corr.reshape(SLOTS, PH, LANES)
            results.append(tuple(totals[j][k] + (corr[k] * scale) * gain[k] for k in range(SLOTS)))
        return tuple(results)

    totals = tuple(tuple(jnp.zeros((PH, LANES), jnp.float32) for _ in range(SLOTS)) for _ in range(tiles))
    gain_copy.wait()

    def part(c, totals):
        span = pl.ds(c * chunk, chunk)
        pltpu.make_async_copy(shifts.at[span], held.at[span], held_sems.at[c]).wait()
        return lax.fori_loop(0, chunk, lambda i, totals: station(c * chunk + i, totals), totals, unroll=True)

    totals = lax.fori_loop(0, stations // chunk, part, totals)

    lane = lane_ids((KB, LANES))
    source = lane % PH * width + lane // PH
    for j in range(tiles):
        for b in range(NB):
            tile = jnp.swapaxes(jnp.stack(totals[j][b * KB : (b + 1) * KB]), 0, 1)
            for at, value in enumerate(swap_groups([tile[p] for p in range(PH)], width)):
                out[j * per_tile + at, b] = jnp.take_along_axis(value, source, axis=1)


def correlate(moved, following, shifts, coef):
    owners, stations, block_len = moved.shape
    tiles = owners * block_len // (LANES * PH)
    chunk = math.gcd(stations, CHUNK)
    return pl.pallas_call(
        functools.partial(correlate_kernel, chunk),
        out_shape=jax.ShapeDtypeStruct((owners, NB, KB, LANES), jnp.float32),
        in_specs=[
            pl.BlockSpec(memory_space=pltpu.VMEM),
            pl.BlockSpec(memory_space=pl.ANY),
            pl.BlockSpec(memory_space=pl.ANY),
            pl.BlockSpec(memory_space=pl.ANY),
        ],
        out_specs=pl.BlockSpec(memory_space=pltpu.VMEM),
        scratch_shapes=[
            pltpu.VMEM(shifts.shape, jnp.bfloat16),
            pltpu.VMEM(coef.shape, jnp.float32),
            pltpu.VMEM(following.shape, jnp.bfloat16),
            pltpu.VMEM((tiles + 1, stations, PH, LANES), jnp.float32),
            pltpu.VMEM((tiles, stations, PH, LANES), jnp.float32),
            pltpu.SemaphoreType.DMA((stations // chunk,)),
            pltpu.SemaphoreType.DMA,
            pltpu.SemaphoreType.DMA,
        ],
        compiler_params=pltpu.CompilerParams(vmem_limit_bytes=VMEM),
        cost_estimate=pl.CostEstimate(flops=1_200_000_000, bytes_accessed=10_000_000, transcendentals=0),
        name="correlate",
    )(moved, *(pltpu.with_memory_space_constraint(v, pltpu.HBM) for v in (following, shifts, coef)))


def shards(records, following, library, template_ids, channel_mask, station_group):
    owners = lax.axis_size("tm")
    block_len = records.shape[1]
    stations = library.shape[1]
    moved = lax.all_to_all(records.reshape(owners, stations, block_len), "tm", split_axis=0, concat_axis=0)
    shifts, coef, after = prepare(template_ids, library, channel_mask, station_group, following)
    partial_sum = correlate(moved, after, shifts, coef)
    parts = lax.all_to_all(
        partial_sum.reshape(owners * NB, KB, block_len), ("tm", "sta"), split_axis=0, concat_axis=0
    )
    return jnp.sum(parts, axis=0)[None]


def solution(mesh):
    placed = (
        P("sta", ("days", "tm")),
        P("sta", "days"),
        P(None, ("sta", "tm"), None),
        P(),
        P(),
        P(),
    )
    return jax.shard_map(
        shards,
        mesh=mesh,
        in_specs=placed,
        out_specs=P("sta", None, ("days", "tm")),
        check_vma=False,
    )
```

```python
import functools
import math

import jax
import jax.numpy as jnp
from jax import lax
from jax.experimental import pallas as pl
from jax.experimental.pallas import tpu as pltpu
from jax.sharding import PartitionSpec as P

W = 256
NB = 2
KB = 8
G = 128
SLOTS = NB * KB
PH = 8
LANES = 128
TAPS = W // PH
PIECES = LANES // TAPS
VMEM = 24 << 20
CHUNK = 64
UNROLL = 32
TURNS = LANES // PH
MADE = (8, 12, 4)

epsilon = 1e-06


def lane_ids(shape):
    return lax.broadcasted_iota(jnp.int32, shape, len(shape) - 1)


def shifted(here, after, by):
    if by == 0:
        return here
    lane = lane_ids(here.shape)
    return pltpu.roll(jnp.where(lane < by, after, here), LANES - by, here.ndim - 1)


def swap_groups(values, width):
    lane = lane_ids(values[0].shape)
    step = len(values) // 2
    while step:
        values = list(values)
        low = lane // (width * step) % 2
        low = (low if values[0].dtype == jnp.float32 else low.astype(jnp.float32).astype(values[0].dtype)) == 0
        for q in range(len(values)):
            if q // step % 2 == 0:
                a, b = values[q], values[q + step]
                values[q] = jnp.where(low, a, pltpu.roll(b, width * step, b.ndim - 1))
                values[q + step] = jnp.where(low, pltpu.roll(a, LANES - width * step, a.ndim - 1), b)
        step //= 2
    return values


def prepare_kernel(
    ids,
    library,
    mask,
    group,
    following,
    shifts,
    coef,
    after,
    edges,
    picked,
    wide,
    rows,
    made,
    gains,
    own_tail,
    edge,
    row_sem,
    in_sem,
    tail_sem,
    out_sem,
    gain_sem,
    edge_sem,
):
    stations = library.shape[1]
    total = mask.shape[1]
    position = lax.axis_index("tm")
    for k in range(SLOTS):
        pltpu.make_async_copy(library.at[ids[k // KB, k % KB]], picked.at[k], in_sem).start()
    for k in range(SLOTS):
        pltpu.make_async_copy(mask.at[pl.ds(ids[k // KB, k % KB], 1)], rows.at[pl.ds(k, 1)], row_sem).start()
    tail_in = pltpu.make_async_copy(following.at[pl.ds(position * stations, stations)], own_tail, tail_sem)
    tail_in.start()

    members = lax.broadcasted_iota(jnp.int32, (G, total), 0) == group[...]
    members = members.astype(jnp.float32).astype(jnp.bfloat16)
    pltpu.make_async_copy(mask.at[pl.ds(0, SLOTS)], rows, row_sem).wait()
    counts = lax.dot_general(
        rows[...].astype(jnp.float32).astype(jnp.bfloat16),
        members,
        (((1,), (1,)), ((), ())),
        preferred_element_type=jnp.float32,
    )
    first = lax.axis_index("sta") * (stations * lax.axis_size("tm")) + position * stations
    block = pl.multiple_of(first // LANES * LANES, LANES)
    own_group = jnp.broadcast_to(group[:, pl.ds(block, LANES)], (G, LANES))
    own_mask = rows[:, pl.ds(block, LANES)].astype(jnp.float32)
    own = (lax.broadcasted_iota(jnp.int32, (G, LANES), 0) == own_group).astype(jnp.float32)
    per_station = jnp.dot(counts, own, preferred_element_type=jnp.float32, precision=lax.Precision.HIGHEST)
    scaled = own_mask / jnp.sqrt(jnp.float32(W * G) * jnp.maximum(per_station, 1.0))
    if stations % LANES:
        scaled = pltpu.roll(scaled, LANES - (first - block), 1)
    scaled = jnp.concatenate([scaled, jnp.zeros((LANES - SLOTS, LANES), jnp.float32)], axis=0).T

    for k in range(SLOTS):
        pltpu.make_async_copy(library.at[0], picked.at[k], in_sem).wait()
    columns = []
    for k in range(SLOTS):
        values = picked[k].astype(jnp.float32)
        wide[k] = values
        tmean = jnp.sum(values * values, axis=1, keepdims=True) / W
        value = scaled[:stations, k : k + 1] / jnp.sqrt(tmean + epsilon)
        columns.append(jnp.broadcast_to(value, (stations, LANES)))
    gains[...] = jnp.swapaxes(jnp.stack(columns), 0, 1)
    gains_out = pltpu.make_async_copy(gains, coef, gain_sem)
    gains_out.start()
    tail_in.wait()
    after[...] = jnp.concatenate([own_tail[...], jnp.zeros((stations, 1), jnp.bfloat16)], axis=1)

    lane = lane_ids((PH, LANES))
    row = lax.broadcasted_iota(jnp.int32, (PH, LANES), 0)

    def part(c, carry):
        rest = [jnp.zeros((PH, LANES), jnp.float32) for _ in range(SLOTS)]
        for i in range(TURNS):
            s = c * TURNS + i
            inside = lane >= row + PH * i
            wrapped = lane < PH * i
            halves = []
            for k in range(SLOTS):
                template = wide[k, pl.ds(s, 1), :]
                turned = [
                    pltpu.roll(
                        jnp.broadcast_to(template[:, h * LANES : (h + 1) * LANES], (PH, LANES)),
                        PH * i,
                        1,
                        stride=1,
                        stride_axis=0,
                    )
                    for h in range(W // LANES)
                ]
                ahead = jnp.where(wrapped, turned[-1], 0.0)
                rest[k] = jnp.where(inside, rest[k], jnp.where(wrapped, rest[k], turned[-1]))
                columns = [jnp.where(inside, turned[h], turned[h - 1] if h else ahead) for h in range(W // LANES)]
                halves.append(jnp.concatenate(columns, axis=1))
            for pair in range(SLOTS // 2):
                value = jnp.concatenate(halves[2 * pair : 2 * pair + 2], axis=0).astype(jnp.bfloat16)
                made[s, 2 * PH * pair : 2 * PH * (pair + 1), :] = value
        edge[c] = jnp.concatenate(rest, axis=0).astype(jnp.bfloat16)
        span = pl.ds(c * TURNS, TURNS)
        pltpu.make_async_copy(made.at[span], shifts.at[span], out_sem).start()
        return carry

    lax.fori_loop(0, stations // TURNS, part, 0)
    edge_out = pltpu.make_async_copy(edge, edges, edge_sem)
    edge_out.start()
    gains_out.wait()
    pltpu.make_async_copy(made, shifts, out_sem).wait()
    edge_out.wait()


def prepare(template_ids, library, channel_mask, station_group, following):
    stations = library.shape[1]
    total = channel_mask.shape[1]
    inputs = template_ids, library, channel_mask, station_group.reshape(1, total), following
    return pl.pallas_call(
        prepare_kernel,
        out_shape=(
            pltpu.HBM((stations, SLOTS * PH, W), jnp.bfloat16),
            pltpu.HBM((stations, SLOTS, LANES), jnp.float32),
            pltpu.VMEM((stations, W), jnp.bfloat16),
            pltpu.HBM((stations // TURNS, SLOTS * PH, LANES), jnp.bfloat16),
        ),
        in_specs=[
            pl.BlockSpec(memory_space=pltpu.SMEM),
            pl.BlockSpec(memory_space=pl.ANY),
            pl.BlockSpec(memory_space=pl.ANY),
            pl.BlockSpec(memory_space=pltpu.VMEM),
            pl.BlockSpec(memory_space=pl.ANY),
        ],
        out_specs=[pl.BlockSpec(memory_space=space) for space in (pl.ANY, pl.ANY, pltpu.VMEM, pl.ANY)],
        scratch_shapes=[
            pltpu.VMEM((SLOTS, stations, W), jnp.bfloat16),
            pltpu.VMEM((SLOTS, stations, W), jnp.float32),
            pltpu.VMEM((SLOTS, total), jnp.int32),
            pltpu.VMEM((stations, SLOTS * PH, W), jnp.bfloat16),
            pltpu.VMEM((stations, SLOTS, LANES), jnp.float32),
            pltpu.VMEM((stations, following.shape[1]), jnp.bfloat16),
            pltpu.VMEM((stations // TURNS, SLOTS * PH, LANES), jnp.bfloat16),
        ]
        + [pltpu.SemaphoreType.DMA] * 6,
        compiler_params=pltpu.CompilerParams(vmem_limit_bytes=VMEM),
        cost_estimate=pl.CostEstimate(flops=10_000_000, bytes_accessed=20_000_000, transcendentals=0),
        name="prepare",
    )(*(pltpu.with_memory_space_constraint(v, pltpu.HBM) for v in inputs))


def correlate_kernel(chunk, moved, following, shifts, coef, edges, out, held, gains, edge, phases, inverse, windows, held_sems, gain_sem, edge_sem):
    owners, stations, block_len = moved.shape
    width = block_len // PH
    tiles = owners * block_len // (LANES * PH)
    per_tile = LANES // width

    def held_copy(c):
        span = pl.ds(c * chunk, chunk)
        return pltpu.make_async_copy(shifts.at[span], held.at[span], held_sems.at[c])

    held_copy(0).start()
    gain_copy = pltpu.make_async_copy(coef, gains, gain_sem)
    gain_copy.start()
    edge_copy = pltpu.make_async_copy(edges, edge, edge_sem)
    edge_copy.start()

    time = lax.broadcasted_iota(jnp.int32, (W, W), 0)
    place = lax.broadcasted_iota(jnp.int32, (W, W), 1)
    order = (time == place % TAPS * PH + place // TAPS).astype(jnp.float32).astype(jnp.bfloat16)

    def split(rows):
        value = jnp.dot(rows, order, preferred_element_type=jnp.float32).astype(jnp.bfloat16)
        return [value[:, h * LANES : (h + 1) * LANES] for h in range(W // LANES)]

    def keep(target, j, parts):
        parts = jnp.stack([v.astype(jnp.float32) for v in parts])
        target[j] = jnp.swapaxes(parts, 0, 1)

    here = (time >= place % TAPS * PH + place // TAPS).astype(jnp.float32).astype(jnp.bfloat16)
    beyond = (time < place % TAPS * PH + place // TAPS).astype(jnp.float32).astype(jnp.bfloat16)

    def squares(rows):
        value = jnp.square(rows.astype(jnp.float32))
        high = value.astype(jnp.bfloat16)
        return high, (value - high.astype(jnp.float32)).astype(jnp.bfloat16)

    each = W // block_len
    rows = [
        jnp.concatenate([moved[q * each + e] for e in range(each)], axis=1) for q in range(tiles * PIECES)
    ]
    for j in range(tiles):
        pieces = [split(r) for r in rows[j * PIECES : (j + 1) * PIECES]]
        keep(phases, j, [v for h in range(PH // PIECES) for v in swap_groups([p[h] for p in pieces], TAPS)])
    rows.append(following[...])
    last = split(rows[-1])
    keep(
        phases,
        tiles,
        [
            pltpu.roll(last[p // PIECES], LANES - TAPS * (p % PIECES), 1) if p % PIECES else last[p // PIECES]
            for p in range(PH)
        ],
    )

    ahead = time - place % LANES - place // LANES
    for parity in range(2):
        for n in range(len(MADE) + 1):
            if n:
                matrix = ahead == 2 * MADE[n - 1] - parity
            else:
                matrix = jnp.logical_and(ahead == TAPS - parity, place // LANES == parity)
            matrix = matrix.astype(jnp.float32).astype(jnp.bfloat16)
            for j in range(tiles):
                value = jnp.concatenate([phases[j], phases[j + 1]], axis=2).reshape(stations // 2, 2, PH, W)[:, parity]
                value = value.reshape(stations // 2 * PH, W).astype(jnp.bfloat16)
                value = jnp.dot(value, matrix, preferred_element_type=jnp.float32)
                value = [value[:, h * LANES : (h + 1) * LANES].reshape(stations // 2, PH, LANES) for h in range(2)]
                windows[n, j, parity] = jnp.concatenate(value, axis=1).astype(jnp.bfloat16)

    squared = [squares(r) for r in rows]
    for j in range(tiles):
        pieces = []
        for q in range(j * PIECES, (j + 1) * PIECES):
            energy = sum(
                jnp.dot(part, matrix, preferred_element_type=jnp.float32)
                for parts, matrix in ((squared[q], here), (squared[q + 1], beyond))
                for part in parts
            )
            energy = lax.rsqrt(energy / W + epsilon)
            pieces.append([energy[:, h * LANES : (h + 1) * LANES] for h in range(W // LANES)])
        keep(inverse, j, [v for h in range(PH // PIECES) for v in swap_groups([p[h] for p in pieces], TAPS)])

    nothing = jnp.zeros((2 * PH, LANES), jnp.bfloat16)

    def window(s, turn, j):
        own, after = phases[j, s], phases[j + 1, s]
        pairs = []
        for i in range(TAPS // 2):
            first = (2 * i - turn) % TAPS
            if (first + 1) // 2 in MADE:
                pairs.append(windows[1 + MADE.index((first + 1) // 2), j, turn % 2, s // 2])
            else:
                pair = [shifted(own, after, by % TAPS) for by in (first, first + 1)]
                pairs.append(jnp.concatenate(pair, axis=0).astype(jnp.bfloat16))
        return jnp.concatenate(pairs, axis=0)

    def two_stations(group, turn, totals):
        s = group * TURNS + turn
        results = []
        for j in range(tiles):
            ends = [
                jnp.concatenate([windows[0, j, e, s // 2] if i == turn // 2 else nothing for i in range(LANES // (2 * PH))], axis=0)
                for e in range(2)
            ]
            ends = jnp.dot(edge[group], jnp.concatenate(ends, axis=1), preferred_element_type=jnp.float32)
            total = totals[j]
            for e in range(2):
                corr = jnp.dot(held[s + e], window(s + e, turn + e, j), preferred_element_type=jnp.float32)
                corr = (corr + ends[:, e * LANES : (e + 1) * LANES]).reshape(SLOTS, PH, LANES)
                scale = inverse[j, s + e]
                gain = [jnp.broadcast_to(gains[s + e, pl.ds(k, 1), :], (PH, LANES)) for k in range(SLOTS)]
                total = tuple(total[k] + (corr[k] * scale) * gain[k] for k in range(SLOTS))
            results.append(total)
        return tuple(results)

    totals = tuple(tuple(jnp.zeros((PH, LANES), jnp.float32) for _ in range(SLOTS)) for _ in range(tiles))
    gain_copy.wait()
    edge_copy.wait()

    def part(c, totals):
        held_copy(c).wait()

        @pl.when(c + 1 < stations // chunk)
        def _():
            held_copy(c + 1).start()

        def some(i, totals):
            for g in range(UNROLL // TURNS):
                for turn in range(0, TURNS, 2):
                    totals = two_stations(c * (chunk // TURNS) + i * (UNROLL // TURNS) + g, turn, totals)
            return totals

        return lax.fori_loop(0, chunk // UNROLL, some, totals)

    totals = lax.fori_loop(0, stations // chunk, part, totals)

    lane = lane_ids((KB, LANES))
    source = lane % PH * width + lane // PH
    for j in range(tiles):
        for b in range(NB):
            tile = jnp.swapaxes(jnp.stack(totals[j][b * KB : (b + 1) * KB]), 0, 1)
            for at, value in enumerate(swap_groups([tile[p] for p in range(PH)], width)):
                out[j * per_tile + at, b] = jnp.take_along_axis(value, source, axis=1)


def correlate(moved, following, shifts, coef, edges):
    owners, stations, block_len = moved.shape
    tiles = owners * block_len // (LANES * PH)
    chunk = math.gcd(stations, CHUNK)
    return pl.pallas_call(
        functools.partial(correlate_kernel, chunk),
        out_shape=jax.ShapeDtypeStruct((owners, NB, KB, LANES), jnp.float32),
        in_specs=[
            pl.BlockSpec(memory_space=pltpu.VMEM),
            pl.BlockSpec(memory_space=pltpu.VMEM),
            pl.BlockSpec(memory_space=pl.ANY),
            pl.BlockSpec(memory_space=pl.ANY),
            pl.BlockSpec(memory_space=pl.ANY),
        ],
        out_specs=pl.BlockSpec(memory_space=pltpu.VMEM),
        scratch_shapes=[
            pltpu.VMEM(shifts.shape, jnp.bfloat16),
            pltpu.VMEM(coef.shape, jnp.float32),
            pltpu.VMEM(edges.shape, jnp.bfloat16),
            pltpu.VMEM((tiles + 1, stations, PH, LANES), jnp.float32),
            pltpu.VMEM((tiles, stations, PH, LANES), jnp.float32),
            pltpu.VMEM((len(MADE) + 1, tiles, 2, stations // 2, 2 * PH, LANES), jnp.bfloat16),
            pltpu.SemaphoreType.DMA((stations // chunk,)),
            pltpu.SemaphoreType.DMA,
            pltpu.SemaphoreType.DMA,
        ],
        compiler_params=pltpu.CompilerParams(vmem_limit_bytes=VMEM),
        cost_estimate=pl.CostEstimate(flops=1_200_000_000, bytes_accessed=10_000_000, transcendentals=0),
        name="correlate",
    )(
        moved,
        pltpu.with_memory_space_constraint(following, pltpu.VMEM),
        *(pltpu.with_memory_space_constraint(v, pltpu.HBM) for v in (shifts, coef, edges)),
    )


def shards(records, following, library, template_ids, channel_mask, station_group):
    owners = lax.axis_size("tm")
    block_len = records.shape[1]
    stations = library.shape[1]
    moved = lax.all_to_all(records.reshape(owners, stations, block_len), "tm", split_axis=0, concat_axis=0)
    shifts, coef, after, edges = prepare(template_ids, library, channel_mask, station_group, following)
    partial_sum = correlate(moved, after, shifts, coef, edges)
    parts = lax.all_to_all(
        partial_sum.reshape(owners * NB, KB, block_len), ("tm", "sta"), split_axis=0, concat_axis=0
    )
    return jnp.sum(parts, axis=0)[None]


def solution(mesh):
    placed = (
        P("sta", ("days", "tm")),
        P("sta", "days"),
        P(None, ("sta", "tm"), None),
        P(),
        P(),
        P(),
    )
    return jax.shard_map(
        shards,
        mesh=mesh,
        in_specs=placed,
        out_specs=P("sta", None, ("days", "tm")),
        check_vma=False,
    )
```

```python
import functools
import math

import jax
import jax.numpy as jnp
from jax import lax
from jax.experimental import pallas as pl
from jax.experimental.pallas import tpu as pltpu
from jax.sharding import PartitionSpec as P

W = 256
NB = 2
KB = 8
G = 128
SLOTS = NB * KB
PH = 8
LANES = 128
TAPS = W // PH
PIECES = LANES // TAPS
VMEM = 24 << 20
CHUNK = 64
AHEAD = 1
UNROLL = 64
TURNS = LANES // PH
MADE = (8, 4)

epsilon = 1e-06


def lane_ids(shape):
    return lax.broadcasted_iota(jnp.int32, shape, len(shape) - 1)


def shifted(here, after, by):
    if by == 0:
        return here
    lane = lane_ids(here.shape)
    return pltpu.roll(jnp.where(lane < by, after, here), LANES - by, here.ndim - 1)


def swap_groups(values, width):
    lane = lane_ids(values[0].shape)
    step = len(values) // 2
    while step:
        values = list(values)
        low = lane // (width * step) % 2
        low = (low if values[0].dtype == jnp.float32 else low.astype(jnp.float32).astype(values[0].dtype)) == 0
        for q in range(len(values)):
            if q // step % 2 == 0:
                a, b = values[q], values[q + step]
                values[q] = jnp.where(low, a, pltpu.roll(b, width * step, b.ndim - 1))
                values[q + step] = jnp.where(low, pltpu.roll(a, LANES - width * step, a.ndim - 1), b)
        step //= 2
    return values


def prepare_kernel(
    ids,
    library,
    mask,
    group,
    following,
    shifts,
    coef,
    after,
    edges,
    picked,
    wide,
    rows,
    made,
    gains,
    own_tail,
    tail,
    edge,
    row_sem,
    in_sem,
    tail_sem,
    out_sem,
    gain_sem,
    after_sem,
    edge_sem,
):
    stations = library.shape[1]
    total = mask.shape[1]
    position = lax.axis_index("tm")
    for k in range(SLOTS):
        pltpu.make_async_copy(library.at[ids[k // KB, k % KB]], picked.at[k], in_sem).start()
    for k in range(SLOTS):
        pltpu.make_async_copy(mask.at[pl.ds(ids[k // KB, k % KB], 1)], rows.at[pl.ds(k, 1)], row_sem).start()
    tail_in = pltpu.make_async_copy(following.at[pl.ds(position * stations, stations)], own_tail, tail_sem)
    tail_in.start()

    for k in range(SLOTS):
        pltpu.make_async_copy(library.at[0], picked.at[k], in_sem).wait()
    for k in range(SLOTS):
        wide[k] = picked[k].astype(jnp.float32)
    tail_in.wait()
    tail[...] = jnp.concatenate([own_tail[...], jnp.zeros((stations, 1), jnp.bfloat16)], axis=1)
    tail_out = pltpu.make_async_copy(tail, after, after_sem)
    tail_out.start()

    lane = lane_ids((PH, LANES))
    row = lax.broadcasted_iota(jnp.int32, (PH, LANES), 0)

    def part(c, carry):
        rest = [jnp.zeros((PH, LANES), jnp.float32) for _ in range(SLOTS)]
        for i in range(TURNS):
            s = c * TURNS + i
            inside = lane >= row + PH * i
            wrapped = lane < PH * i
            halves = []
            for k in range(SLOTS):
                template = wide[k, pl.ds(s, 1), :]
                turned = [
                    pltpu.roll(
                        jnp.broadcast_to(template[:, h * LANES : (h + 1) * LANES], (PH, LANES)),
                        PH * i,
                        1,
                        stride=1,
                        stride_axis=0,
                    )
                    for h in range(W // LANES)
                ]
                ahead = jnp.where(wrapped, turned[-1], 0.0)
                rest[k] = jnp.where(inside, rest[k], jnp.where(wrapped, rest[k], turned[-1]))
                columns = [jnp.where(inside, turned[h], turned[h - 1] if h else ahead) for h in range(W // LANES)]
                halves.append(jnp.concatenate(columns, axis=1))
            for pair in range(SLOTS // 2):
                value = jnp.concatenate(halves[2 * pair : 2 * pair + 2], axis=0).astype(jnp.bfloat16)
                made[s, 2 * PH * pair : 2 * PH * (pair + 1), :] = value
        edge[c] = jnp.concatenate(rest, axis=0).astype(jnp.bfloat16)
        span = pl.ds(c * TURNS, TURNS)
        pltpu.make_async_copy(made.at[span], shifts.at[span], out_sem).start()
        return carry

    lax.fori_loop(0, stations // TURNS, part, 0)
    edge_out = pltpu.make_async_copy(edge, edges, edge_sem)
    edge_out.start()

    members = lax.broadcasted_iota(jnp.int32, (G, total), 0) == group[...]
    members = members.astype(jnp.float32).astype(jnp.bfloat16)
    pltpu.make_async_copy(mask.at[pl.ds(0, SLOTS)], rows, row_sem).wait()
    counts = lax.dot_general(
        rows[...].astype(jnp.float32).astype(jnp.bfloat16),
        members,
        (((1,), (1,)), ((), ())),
        preferred_element_type=jnp.float32,
    )
    first = lax.axis_index("sta") * (stations * lax.axis_size("tm")) + position * stations
    block = pl.multiple_of(first // LANES * LANES, LANES)
    own_group = jnp.broadcast_to(group[:, pl.ds(block, LANES)], (G, LANES))
    own_mask = rows[:, pl.ds(block, LANES)].astype(jnp.float32)
    own = (lax.broadcasted_iota(jnp.int32, (G, LANES), 0) == own_group).astype(jnp.float32)
    per_station = jnp.dot(counts, own, preferred_element_type=jnp.float32, precision=lax.Precision.HIGHEST)
    scaled = own_mask / jnp.sqrt(jnp.float32(W * G) * jnp.maximum(per_station, 1.0))
    if stations % LANES:
        scaled = pltpu.roll(scaled, LANES - (first - block), 1)
    sums = jnp.zeros((stations, LANES), jnp.float32)
    for k in range(SLOTS):
        values = jnp.square(wide[k])
        values = sum(values[:, h * LANES : (h + 1) * LANES] for h in range(W // LANES))
        high = values.astype(jnp.bfloat16)
        low = (values - high.astype(jnp.float32)).astype(jnp.bfloat16)
        column = (lane_ids((LANES, LANES)) == k).astype(jnp.float32).astype(jnp.bfloat16)
        sums = sums + jnp.dot(high, column, preferred_element_type=jnp.float32)
        sums = sums + jnp.dot(low, column, preferred_element_type=jnp.float32)
    if stations < LANES:
        sums = jnp.concatenate([sums, jnp.zeros((LANES - stations, LANES), jnp.float32)], axis=0)
    gains[...] = scaled / jnp.sqrt(sums.T[:SLOTS] / W + epsilon)
    gains_out = pltpu.make_async_copy(gains, coef, gain_sem)
    gains_out.start()

    gains_out.wait()
    tail_out.wait()
    pltpu.make_async_copy(made, shifts, out_sem).wait()
    edge_out.wait()


def prepare(template_ids, library, channel_mask, station_group, following):
    stations = library.shape[1]
    total = channel_mask.shape[1]
    inputs = template_ids, library, channel_mask, station_group.reshape(1, total), following
    return pl.pallas_call(
        prepare_kernel,
        out_shape=(
            pltpu.HBM((stations, SLOTS * PH, W), jnp.bfloat16),
            pltpu.HBM((SLOTS, LANES), jnp.float32),
            pltpu.HBM((stations, W), jnp.bfloat16),
            pltpu.HBM((stations // TURNS, SLOTS * PH, LANES), jnp.bfloat16),
        ),
        in_specs=[
            pl.BlockSpec(memory_space=pltpu.SMEM),
            pl.BlockSpec(memory_space=pl.ANY),
            pl.BlockSpec(memory_space=pl.ANY),
            pl.BlockSpec(memory_space=pltpu.VMEM),
            pl.BlockSpec(memory_space=pl.ANY),
        ],
        out_specs=[pl.BlockSpec(memory_space=pl.ANY)] * 4,
        scratch_shapes=[
            pltpu.VMEM((SLOTS, stations, W), jnp.bfloat16),
            pltpu.VMEM((SLOTS, stations, W), jnp.float32),
            pltpu.VMEM((SLOTS, total), jnp.int32),
            pltpu.VMEM((stations, SLOTS * PH, W), jnp.bfloat16),
            pltpu.VMEM((SLOTS, LANES), jnp.float32),
            pltpu.VMEM((stations, following.shape[1]), jnp.bfloat16),
            pltpu.VMEM((stations, W), jnp.bfloat16),
            pltpu.VMEM((stations // TURNS, SLOTS * PH, LANES), jnp.bfloat16),
        ]
        + [pltpu.SemaphoreType.DMA] * 7,
        compiler_params=pltpu.CompilerParams(vmem_limit_bytes=VMEM),
        cost_estimate=pl.CostEstimate(flops=10_000_000, bytes_accessed=20_000_000, transcendentals=0),
        name="prepare",
    )(*(pltpu.with_memory_space_constraint(v, pltpu.HBM) for v in inputs))


def correlate_kernel(chunk, moved, following, shifts, coef, edges, out, held, gains, edge, tail, phases, inverse, windows, held_sems, gain_sem, edge_sem, tail_sem):
    owners, stations, block_len = moved.shape
    width = block_len // PH
    tiles = owners * block_len // (LANES * PH)
    per_tile = LANES // width

    tail_copy = pltpu.make_async_copy(following, tail, tail_sem)
    tail_copy.start()
    def held_copy(c):
        span = pl.ds(c * chunk, chunk)
        return pltpu.make_async_copy(shifts.at[span], held.at[span], held_sems.at[c])

    gain_copy = pltpu.make_async_copy(coef, gains, gain_sem)
    gain_copy.start()
    edge_copy = pltpu.make_async_copy(edges, edge, edge_sem)
    edge_copy.start()
    for c in range(min(AHEAD, stations // chunk)):
        held_copy(c).start()

    time = lax.broadcasted_iota(jnp.int32, (W, W), 0)
    place = lax.broadcasted_iota(jnp.int32, (W, W), 1)
    order = (time == place % TAPS * PH + place // TAPS).astype(jnp.float32).astype(jnp.bfloat16)

    def split(rows):
        value = jnp.dot(rows, order, preferred_element_type=jnp.float32).astype(jnp.bfloat16)
        return [value[:, h * LANES : (h + 1) * LANES] for h in range(W // LANES)]

    def keep(target, j, parts):
        parts = jnp.stack([v.astype(jnp.float32) for v in parts])
        target[j] = jnp.swapaxes(parts, 0, 1)

    here = (time >= place % TAPS * PH + place // TAPS).astype(jnp.float32).astype(jnp.bfloat16)
    beyond = (time < place % TAPS * PH + place // TAPS).astype(jnp.float32).astype(jnp.bfloat16)

    def squares(rows):
        value = jnp.square(rows.astype(jnp.float32))
        high = value.astype(jnp.bfloat16)
        return high, (value - high.astype(jnp.float32)).astype(jnp.bfloat16)

    each = W // block_len
    rows = [
        jnp.concatenate([moved[q * each + e] for e in range(each)], axis=1) for q in range(tiles * PIECES)
    ]
    for j in range(tiles):
        pieces = [split(r) for r in rows[j * PIECES : (j + 1) * PIECES]]
        keep(phases, j, [v for h in range(PH // PIECES) for v in swap_groups([p[h] for p in pieces], TAPS)])
    tail_copy.wait()
    rows.append(tail[...])
    last = split(rows[-1])
    keep(
        phases,
        tiles,
        [
            pltpu.roll(last[p // PIECES], LANES - TAPS * (p % PIECES), 1) if p % PIECES else last[p // PIECES]
            for p in range(PH)
        ],
    )

    ahead = time - place % LANES - place // LANES
    for parity in range(2):
        for n in range(len(MADE) + 1):
            if n:
                matrix = ahead == 2 * MADE[n - 1] - parity
            else:
                matrix = jnp.logical_and(ahead == TAPS - parity, place // LANES == parity)
            matrix = matrix.astype(jnp.float32).astype(jnp.bfloat16)
            for j in range(tiles):
                value = jnp.concatenate([phases[j], phases[j + 1]], axis=2).reshape(stations // 2, 2, PH, W)[:, parity]
                value = value.reshape(stations // 2 * PH, W).astype(jnp.bfloat16)
                value = jnp.dot(value, matrix, preferred_element_type=jnp.float32)
                value = [value[:, h * LANES : (h + 1) * LANES].reshape(stations // 2, PH, LANES) for h in range(2)]
                windows[n, j, parity] = jnp.concatenate(value, axis=1).astype(jnp.bfloat16)

    squared = [squares(r) for r in rows]
    for j in range(tiles):
        pieces = []
        for q in range(j * PIECES, (j + 1) * PIECES):
            energy = sum(
                jnp.dot(part, matrix, preferred_element_type=jnp.float32)
                for parts, matrix in ((squared[q], here), (squared[q + 1], beyond))
                for part in parts
            )
            energy = lax.rsqrt(energy / W + epsilon)
            pieces.append([energy[:, h * LANES : (h + 1) * LANES] for h in range(W // LANES)])
        keep(inverse, j, [v for h in range(PH // PIECES) for v in swap_groups([p[h] for p in pieces], TAPS)])

    nothing = jnp.zeros((2 * PH, LANES), jnp.bfloat16)

    def window(s, turn, j):
        own, after = phases[j, s], phases[j + 1, s]
        pairs = []
        for i in range(TAPS // 2):
            first = (2 * i - turn) % TAPS
            if (first + 1) // 2 in MADE:
                pairs.append(windows[1 + MADE.index((first + 1) // 2), j, turn % 2, s // 2])
            else:
                pair = [shifted(own, after, by % TAPS) for by in (first, first + 1)]
                pairs.append(jnp.concatenate(pair, axis=0).astype(jnp.bfloat16))
        return jnp.concatenate(pairs, axis=0)

    def two_stations(group, turn, totals):
        s = group * TURNS + turn
        results = []
        for j in range(tiles):
            ends = [
                jnp.concatenate([windows[0, j, e, s // 2] if i == turn // 2 else nothing for i in range(LANES // (2 * PH))], axis=0)
                for e in range(2)
            ]
            ends = jnp.dot(edge[group], jnp.concatenate(ends, axis=1), preferred_element_type=jnp.float32)
            total = totals[j]
            for e in range(2):
                corr = jnp.dot(held[s + e], window(s + e, turn + e, j), preferred_element_type=jnp.float32)
                corr = (corr + ends[:, e * LANES : (e + 1) * LANES]).reshape(SLOTS, PH, LANES)
                scale = inverse[j, s + e]
                total = tuple(total[k] + (corr[k] * scale) * gains[k, s + e] for k in range(SLOTS))
            results.append(total)
        return tuple(results)

    totals = tuple(tuple(jnp.zeros((PH, LANES), jnp.float32) for _ in range(SLOTS)) for _ in range(tiles))
    gain_copy.wait()
    edge_copy.wait()

    block = min(UNROLL, chunk)

    def part(c, totals):
        held_copy(c).wait()

        @pl.when(c + AHEAD < stations // chunk)
        def _():
            held_copy(c + AHEAD).start()

        def some(i, totals):
            for g in range(block // TURNS):
                for turn in range(0, TURNS, 2):
                    totals = two_stations(c * (chunk // TURNS) + i * (block // TURNS) + g, turn, totals)
            return totals

        return lax.fori_loop(0, chunk // block, some, totals)

    totals = lax.fori_loop(0, stations // chunk, part, totals)

    lane = lane_ids((KB, LANES))
    source = lane % PH * width + lane // PH
    for j in range(tiles):
        for b in range(NB):
            tile = jnp.swapaxes(jnp.stack(totals[j][b * KB : (b + 1) * KB]), 0, 1)
            for at, value in enumerate(swap_groups([tile[p] for p in range(PH)], width)):
                out[j * per_tile + at, b] = jnp.take_along_axis(value, source, axis=1)


def correlate(moved, following, shifts, coef, edges):
    owners, stations, block_len = moved.shape
    tiles = owners * block_len // (LANES * PH)
    chunk = math.gcd(stations, CHUNK)
    return pl.pallas_call(
        functools.partial(correlate_kernel, chunk),
        out_shape=jax.ShapeDtypeStruct((owners, NB, KB, LANES), jnp.float32),
        in_specs=[
            pl.BlockSpec(memory_space=pltpu.VMEM),
            pl.BlockSpec(memory_space=pl.ANY),
            pl.BlockSpec(memory_space=pl.ANY),
            pl.BlockSpec(memory_space=pl.ANY),
            pl.BlockSpec(memory_space=pl.ANY),
        ],
        out_specs=pl.BlockSpec(memory_space=pltpu.VMEM),
        scratch_shapes=[
            pltpu.VMEM(shifts.shape, jnp.bfloat16),
            pltpu.SMEM(coef.shape, jnp.float32),
            pltpu.VMEM(edges.shape, jnp.bfloat16),
            pltpu.VMEM(following.shape, jnp.bfloat16),
            pltpu.VMEM((tiles + 1, stations, PH, LANES), jnp.float32),
            pltpu.VMEM((tiles, stations, PH, LANES), jnp.float32),
            pltpu.VMEM((len(MADE) + 1, tiles, 2, stations // 2, 2 * PH, LANES), jnp.bfloat16),
            pltpu.SemaphoreType.DMA((stations // chunk,)),
            pltpu.SemaphoreType.DMA,
            pltpu.SemaphoreType.DMA,
            pltpu.SemaphoreType.DMA,
        ],
        compiler_params=pltpu.CompilerParams(vmem_limit_bytes=VMEM),
        cost_estimate=pl.CostEstimate(flops=1_200_000_000, bytes_accessed=10_000_000, transcendentals=0),
        name="correlate",
    )(moved, *(pltpu.with_memory_space_constraint(v, pltpu.HBM) for v in (following, shifts, coef, edges)))


def shards(records, following, library, template_ids, channel_mask, station_group):
    owners = lax.axis_size("tm")
    block_len = records.shape[1]
    stations = library.shape[1]
    moved = lax.all_to_all(records.reshape(owners, stations, block_len), "tm", split_axis=0, concat_axis=0)
    shifts, coef, after, edges = prepare(template_ids, library, channel_mask, station_group, following)
    partial_sum = correlate(moved, after, shifts, coef, edges)
    parts = lax.all_to_all(
        partial_sum.reshape(owners * NB, KB, block_len), ("tm", "sta"), split_axis=0, concat_axis=0
    )
    return jnp.sum(parts, axis=0)[None]


def solution(mesh):
    placed = (
        P("sta", ("days", "tm")),
        P("sta", "days"),
        P(None, ("sta", "tm"), None),
        P(),
        P(),
        P(),
    )
    return jax.shard_map(
        shards,
        mesh=mesh,
        in_specs=placed,
        out_specs=P("sta", None, ("days", "tm")),
        check_vma=False,
    )
```

```python
import functools

import jax
import jax.numpy as jnp
from jax import lax
from jax.experimental import pallas as pl
from jax.experimental.pallas import tpu as pltpu
from jax.sharding import PartitionSpec as P

W = 256
NB = 2
KB = 8
G = 128
SLOTS = NB * KB
PH = 8
LANES = 128
TAPS = W // PH
PIECES = LANES // TAPS
VMEM = 24 << 20
PARTS = (48, 80)
START = (0, 1)
TURNS = LANES // PH
MADE = (8, 4)

epsilon = 1e-06


def lane_ids(shape):
    return lax.broadcasted_iota(jnp.int32, shape, len(shape) - 1)


def shifted(here, after, by):
    if by == 0:
        return here
    lane = lane_ids(here.shape)
    return pltpu.roll(jnp.where(lane < by, after, here), LANES - by, here.ndim - 1)


def swap_groups(values, width):
    lane = lane_ids(values[0].shape)
    step = len(values) // 2
    while step:
        values = list(values)
        low = lane // (width * step) % 2
        low = (low if values[0].dtype == jnp.float32 else low.astype(jnp.float32).astype(values[0].dtype)) == 0
        for q in range(len(values)):
            if q // step % 2 == 0:
                a, b = values[q], values[q + step]
                values[q] = jnp.where(low, a, pltpu.roll(b, width * step, b.ndim - 1))
                values[q + step] = jnp.where(low, pltpu.roll(a, LANES - width * step, a.ndim - 1), b)
        step //= 2
    return values


def prepare_kernel(
    ids,
    library,
    mask,
    group,
    following,
    shifts,
    coef,
    after,
    edges,
    picked,
    wide,
    rows,
    made,
    gains,
    own_tail,
    tail,
    edge,
    row_sem,
    in_sem,
    tail_sem,
    out_sem,
    gain_sem,
    after_sem,
    edge_sem,
):
    stations = library.shape[1]
    total = mask.shape[1]
    position = lax.axis_index("tm")
    for k in range(SLOTS):
        pltpu.make_async_copy(library.at[ids[k // KB, k % KB]], picked.at[k], in_sem).start()
    for k in range(SLOTS):
        pltpu.make_async_copy(mask.at[pl.ds(ids[k // KB, k % KB], 1)], rows.at[pl.ds(k, 1)], row_sem).start()
    tail_in = pltpu.make_async_copy(following.at[pl.ds(position * stations, stations)], own_tail, tail_sem)
    tail_in.start()

    for k in range(SLOTS):
        pltpu.make_async_copy(library.at[0], picked.at[k], in_sem).wait()
    for k in range(SLOTS):
        wide[k] = picked[k].astype(jnp.float32)
    tail_in.wait()
    tail[...] = jnp.concatenate([own_tail[...], jnp.zeros((stations, 1), jnp.bfloat16)], axis=1)
    tail_out = pltpu.make_async_copy(tail, after, after_sem)
    tail_out.start()

    lane = lane_ids((PH, LANES))
    row = lax.broadcasted_iota(jnp.int32, (PH, LANES), 0)

    def part(c, carry):
        rest = [jnp.zeros((PH, LANES), jnp.float32) for _ in range(SLOTS)]
        for i in range(TURNS):
            s = c * TURNS + i
            inside = lane >= row + PH * i
            wrapped = lane < PH * i
            halves = []
            for k in range(SLOTS):
                template = wide[k, pl.ds(s, 1), :]
                turned = [
                    pltpu.roll(
                        jnp.broadcast_to(template[:, h * LANES : (h + 1) * LANES], (PH, LANES)),
                        PH * i,
                        1,
                        stride=1,
                        stride_axis=0,
                    )
                    for h in range(W // LANES)
                ]
                ahead = jnp.where(wrapped, turned[-1], 0.0)
                rest[k] = jnp.where(inside, rest[k], jnp.where(wrapped, rest[k], turned[-1]))
                columns = [jnp.where(inside, turned[h], turned[h - 1] if h else ahead) for h in range(W // LANES)]
                halves.append(jnp.concatenate(columns, axis=1))
            for pair in range(SLOTS // 2):
                value = jnp.concatenate(halves[2 * pair : 2 * pair + 2], axis=0).astype(jnp.bfloat16)
                made[s, 2 * PH * pair : 2 * PH * (pair + 1), :] = value
        edge[c] = jnp.concatenate(rest, axis=0).astype(jnp.bfloat16)
        span = pl.ds(c * TURNS, TURNS)
        pltpu.make_async_copy(made.at[span], shifts.at[span], out_sem).start()
        return carry

    lax.fori_loop(0, stations // TURNS, part, 0)
    edge_out = pltpu.make_async_copy(edge, edges, edge_sem)
    edge_out.start()

    members = lax.broadcasted_iota(jnp.int32, (G, total), 0) == group[...]
    members = members.astype(jnp.float32).astype(jnp.bfloat16)
    pltpu.make_async_copy(mask.at[pl.ds(0, SLOTS)], rows, row_sem).wait()
    counts = lax.dot_general(
        rows[...].astype(jnp.float32).astype(jnp.bfloat16),
        members,
        (((1,), (1,)), ((), ())),
        preferred_element_type=jnp.float32,
    )
    first = lax.axis_index("sta") * (stations * lax.axis_size("tm")) + position * stations
    block = pl.multiple_of(first // LANES * LANES, LANES)
    own_group = jnp.broadcast_to(group[:, pl.ds(block, LANES)], (G, LANES))
    own_mask = rows[:, pl.ds(block, LANES)].astype(jnp.float32)
    own = (lax.broadcasted_iota(jnp.int32, (G, LANES), 0) == own_group).astype(jnp.float32)
    per_station = jnp.dot(counts, own, preferred_element_type=jnp.float32, precision=lax.Precision.HIGHEST)
    scaled = own_mask / jnp.sqrt(jnp.float32(W * G) * jnp.maximum(per_station, 1.0))
    if stations % LANES:
        scaled = pltpu.roll(scaled, LANES - (first - block), 1)
    sums = jnp.zeros((stations, LANES), jnp.float32)
    for k in range(SLOTS):
        values = jnp.square(wide[k])
        values = sum(values[:, h * LANES : (h + 1) * LANES] for h in range(W // LANES))
        high = values.astype(jnp.bfloat16)
        low = (values - high.astype(jnp.float32)).astype(jnp.bfloat16)
        column = (lane_ids((LANES, LANES)) == k).astype(jnp.float32).astype(jnp.bfloat16)
        sums = sums + jnp.dot(high, column, preferred_element_type=jnp.float32)
        sums = sums + jnp.dot(low, column, preferred_element_type=jnp.float32)
    if stations < LANES:
        sums = jnp.concatenate([sums, jnp.zeros((LANES - stations, LANES), jnp.float32)], axis=0)
    gains[...] = scaled / jnp.sqrt(sums.T[:SLOTS] / W + epsilon)
    gains_out = pltpu.make_async_copy(gains, coef, gain_sem)
    gains_out.start()

    gains_out.wait()
    tail_out.wait()
    pltpu.make_async_copy(made, shifts, out_sem).wait()
    edge_out.wait()


def prepare(template_ids, library, channel_mask, station_group, following):
    stations = library.shape[1]
    total = channel_mask.shape[1]
    inputs = template_ids, library, channel_mask, station_group.reshape(1, total), following
    return pl.pallas_call(
        prepare_kernel,
        out_shape=(
            pltpu.HBM((stations, SLOTS * PH, W), jnp.bfloat16),
            pltpu.HBM((SLOTS, LANES), jnp.float32),
            pltpu.HBM((stations, W), jnp.bfloat16),
            pltpu.HBM((stations // TURNS, SLOTS * PH, LANES), jnp.bfloat16),
        ),
        in_specs=[
            pl.BlockSpec(memory_space=pltpu.SMEM),
            pl.BlockSpec(memory_space=pl.ANY),
            pl.BlockSpec(memory_space=pl.ANY),
            pl.BlockSpec(memory_space=pltpu.VMEM),
            pl.BlockSpec(memory_space=pl.ANY),
        ],
        out_specs=[pl.BlockSpec(memory_space=pl.ANY)] * 4,
        scratch_shapes=[
            pltpu.VMEM((SLOTS, stations, W), jnp.bfloat16),
            pltpu.VMEM((SLOTS, stations, W), jnp.float32),
            pltpu.VMEM((SLOTS, total), jnp.int32),
            pltpu.VMEM((stations, SLOTS * PH, W), jnp.bfloat16),
            pltpu.VMEM((SLOTS, LANES), jnp.float32),
            pltpu.VMEM((stations, following.shape[1]), jnp.bfloat16),
            pltpu.VMEM((stations, W), jnp.bfloat16),
            pltpu.VMEM((stations // TURNS, SLOTS * PH, LANES), jnp.bfloat16),
        ]
        + [pltpu.SemaphoreType.DMA] * 7,
        compiler_params=pltpu.CompilerParams(vmem_limit_bytes=VMEM),
        cost_estimate=pl.CostEstimate(flops=10_000_000, bytes_accessed=20_000_000, transcendentals=0),
        name="prepare",
    )(*(pltpu.with_memory_space_constraint(v, pltpu.HBM) for v in inputs))


def correlate_kernel(moved, following, shifts, coef, edges, out, held, gains, edge, tail, phases, inverse, windows, held_sems, gain_sem, edge_sem, tail_sem):
    owners, stations, block_len = moved.shape
    width = block_len // PH
    tiles = owners * block_len // (LANES * PH)
    per_tile = LANES // width

    tail_copy = pltpu.make_async_copy(following, tail, tail_sem)
    tail_copy.start()
    bounds = [0]
    for size in PARTS:
        bounds.append(min(stations, bounds[-1] + size))
    bounds[-1] = stations

    def held_copies(stage):
        for n, when in enumerate(START):
            if when == stage and bounds[n] < bounds[n + 1]:
                held_copy(n).start()

    def held_copy(n):
        span = pl.ds(bounds[n], bounds[n + 1] - bounds[n])
        return pltpu.make_async_copy(shifts.at[span], held.at[span], held_sems.at[n])

    gain_copy = pltpu.make_async_copy(coef, gains, gain_sem)
    gain_copy.start()
    edge_copy = pltpu.make_async_copy(edges, edge, edge_sem)
    edge_copy.start()
    held_copies(0)

    time = lax.broadcasted_iota(jnp.int32, (W, W), 0)
    place = lax.broadcasted_iota(jnp.int32, (W, W), 1)
    order = (time == place % TAPS * PH + place // TAPS).astype(jnp.float32).astype(jnp.bfloat16)

    def split(rows):
        value = jnp.dot(rows, order, preferred_element_type=jnp.float32).astype(jnp.bfloat16)
        return [value[:, h * LANES : (h + 1) * LANES] for h in range(W // LANES)]

    def keep(target, j, parts):
        parts = jnp.stack([v.astype(jnp.float32) for v in parts])
        target[j] = jnp.swapaxes(parts, 0, 1)

    here = (time >= place % TAPS * PH + place // TAPS).astype(jnp.float32).astype(jnp.bfloat16)
    beyond = (time < place % TAPS * PH + place // TAPS).astype(jnp.float32).astype(jnp.bfloat16)

    def squares(rows):
        value = jnp.square(rows.astype(jnp.float32))
        high = value.astype(jnp.bfloat16)
        return high, (value - high.astype(jnp.float32)).astype(jnp.bfloat16)

    each = W // block_len
    rows = [
        jnp.concatenate([moved[q * each + e] for e in range(each)], axis=1) for q in range(tiles * PIECES)
    ]
    for j in range(tiles):
        pieces = [split(r) for r in rows[j * PIECES : (j + 1) * PIECES]]
        keep(phases, j, [v for h in range(PH // PIECES) for v in swap_groups([p[h] for p in pieces], TAPS)])
    tail_copy.wait()
    rows.append(tail[...])
    last = split(rows[-1])
    keep(
        phases,
        tiles,
        [
            pltpu.roll(last[p // PIECES], LANES - TAPS * (p % PIECES), 1) if p % PIECES else last[p // PIECES]
            for p in range(PH)
        ],
    )

    held_copies(1)

    ahead = time - place % LANES - place // LANES
    for parity in range(2):
        for n in range(len(MADE) + 1):
            if n:
                matrix = ahead == 2 * MADE[n - 1] - parity
            else:
                matrix = jnp.logical_and(ahead == TAPS - parity, place // LANES == parity)
            matrix = matrix.astype(jnp.float32).astype(jnp.bfloat16)
            for j in range(tiles):
                value = jnp.concatenate([phases[j], phases[j + 1]], axis=2).reshape(stations // 2, 2, PH, W)[:, parity]
                value = value.reshape(stations // 2 * PH, W).astype(jnp.bfloat16)
                value = jnp.dot(value, matrix, preferred_element_type=jnp.float32)
                value = [value[:, h * LANES : (h + 1) * LANES].reshape(stations // 2, PH, LANES) for h in range(2)]
                windows[n, j, parity] = jnp.concatenate(value, axis=1).astype(jnp.bfloat16)

    squared = [squares(r) for r in rows]
    for j in range(tiles):
        pieces = []
        for q in range(j * PIECES, (j + 1) * PIECES):
            energy = sum(
                jnp.dot(part, matrix, preferred_element_type=jnp.float32)
                for parts, matrix in ((squared[q], here), (squared[q + 1], beyond))
                for part in parts
            )
            energy = lax.rsqrt(energy / W + epsilon)
            pieces.append([energy[:, h * LANES : (h + 1) * LANES] for h in range(W // LANES)])
        keep(inverse, j, [v for h in range(PH // PIECES) for v in swap_groups([p[h] for p in pieces], TAPS)])

    nothing = jnp.zeros((2 * PH, LANES), jnp.bfloat16)

    def window(s, turn, j):
        own, after = phases[j, s], phases[j + 1, s]
        pairs = []
        for i in range(TAPS // 2):
            first = (2 * i - turn) % TAPS
            if (first + 1) // 2 in MADE:
                pairs.append(windows[1 + MADE.index((first + 1) // 2), j, turn % 2, s // 2])
            else:
                pair = [shifted(own, after, by % TAPS) for by in (first, first + 1)]
                pairs.append(jnp.concatenate(pair, axis=0).astype(jnp.bfloat16))
        return jnp.concatenate(pairs, axis=0)

    def two_stations(group, turn, totals):
        s = group * TURNS + turn
        results = []
        for j in range(tiles):
            ends = [
                jnp.concatenate([windows[0, j, e, s // 2] if i == turn // 2 else nothing for i in range(LANES // (2 * PH))], axis=0)
                for e in range(2)
            ]
            ends = jnp.dot(edge[group], jnp.concatenate(ends, axis=1), preferred_element_type=jnp.float32)
            total = totals[j]
            for e in range(2):
                corr = jnp.dot(held[s + e], window(s + e, turn + e, j), preferred_element_type=jnp.float32)
                corr = (corr + ends[:, e * LANES : (e + 1) * LANES]).reshape(SLOTS, PH, LANES)
                scale = inverse[j, s + e]
                total = tuple(total[k] + (corr[k] * scale) * gains[k, s + e] for k in range(SLOTS))
            results.append(total)
        return tuple(results)

    totals = tuple(tuple(jnp.zeros((PH, LANES), jnp.float32) for _ in range(SLOTS)) for _ in range(tiles))
    gain_copy.wait()
    edge_copy.wait()

    for n in range(len(PARTS)):
        if bounds[n] < bounds[n + 1]:
            if n == 0:
                held_copies(2)
            held_copy(n).wait()
            held_copies(3 + n)
            for s in range(bounds[n], bounds[n + 1], 2):
                totals = two_stations(s // TURNS, s % TURNS, totals)

    lane = lane_ids((KB, LANES))
    source = lane % PH * width + lane // PH
    for j in range(tiles):
        for b in range(NB):
            tile = jnp.swapaxes(jnp.stack(totals[j][b * KB : (b + 1) * KB]), 0, 1)
            for at, value in enumerate(swap_groups([tile[p] for p in range(PH)], width)):
                out[j * per_tile + at, b] = jnp.take_along_axis(value, source, axis=1)


def correlate(moved, following, shifts, coef, edges):
    owners, stations, block_len = moved.shape
    tiles = owners * block_len // (LANES * PH)
    return pl.pallas_call(
        correlate_kernel,
        out_shape=jax.ShapeDtypeStruct((owners, NB, KB, LANES), jnp.float32),
        in_specs=[
            pl.BlockSpec(memory_space=pltpu.VMEM),
            pl.BlockSpec(memory_space=pl.ANY),
            pl.BlockSpec(memory_space=pl.ANY),
            pl.BlockSpec(memory_space=pl.ANY),
            pl.BlockSpec(memory_space=pl.ANY),
        ],
        out_specs=pl.BlockSpec(memory_space=pltpu.VMEM),
        scratch_shapes=[
            pltpu.VMEM(shifts.shape, jnp.bfloat16),
            pltpu.SMEM(coef.shape, jnp.float32),
            pltpu.VMEM(edges.shape, jnp.bfloat16),
            pltpu.VMEM(following.shape, jnp.bfloat16),
            pltpu.VMEM((tiles + 1, stations, PH, LANES), jnp.float32),
            pltpu.VMEM((tiles, stations, PH, LANES), jnp.float32),
            pltpu.VMEM((len(MADE) + 1, tiles, 2, stations // 2, 2 * PH, LANES), jnp.bfloat16),
            pltpu.SemaphoreType.DMA((len(PARTS),)),
            pltpu.SemaphoreType.DMA,
            pltpu.SemaphoreType.DMA,
            pltpu.SemaphoreType.DMA,
        ],
        compiler_params=pltpu.CompilerParams(vmem_limit_bytes=VMEM),
        cost_estimate=pl.CostEstimate(flops=1_200_000_000, bytes_accessed=10_000_000, transcendentals=0),
        name="correlate",
    )(moved, *(pltpu.with_memory_space_constraint(v, pltpu.HBM) for v in (following, shifts, coef, edges)))


def shards(records, following, library, template_ids, channel_mask, station_group):
    owners = lax.axis_size("tm")
    block_len = records.shape[1]
    stations = library.shape[1]
    moved = lax.all_to_all(records.reshape(owners, stations, block_len), "tm", split_axis=0, concat_axis=0)
    shifts, coef, after, edges = prepare(template_ids, library, channel_mask, station_group, following)
    partial_sum = correlate(moved, after, shifts, coef, edges)
    parts = lax.all_to_all(
        partial_sum.reshape(owners * NB, KB, block_len), ("tm", "sta"), split_axis=0, concat_axis=0
    )
    return jnp.sum(parts, axis=0)[None]


def solution(mesh):
    placed = (
        P("sta", ("days", "tm")),
        P("sta", "days"),
        P(None, ("sta", "tm"), None),
        P(),
        P(),
        P(),
    )
    return jax.shard_map(
        shards,
        mesh=mesh,
        in_specs=placed,
        out_specs=P("sta", None, ("days", "tm")),
        check_vma=False,
    )
```

```python
import functools

import jax
import jax.numpy as jnp
from jax import lax
from jax.experimental import pallas as pl
from jax.experimental.pallas import tpu as pltpu
from jax.sharding import PartitionSpec as P

W = 256
NB = 2
KB = 8
G = 128
SLOTS = NB * KB
PH = 8
LANES = 128
TAPS = W // PH
PIECES = LANES // TAPS
VMEM = 24 << 20
PARTS = (48, 80)
START = (0, 1)
TURNS = LANES // PH
MADE = (8, 4)

epsilon = 1e-06


def lane_ids(shape):
    return lax.broadcasted_iota(jnp.int32, shape, len(shape) - 1)


def shifted(here, after, by):
    if by == 0:
        return here
    lane = lane_ids(here.shape)
    return pltpu.roll(jnp.where(lane < by, after, here), LANES - by, here.ndim - 1)


def swap_groups(values, width):
    lane = lane_ids(values[0].shape)
    step = len(values) // 2
    while step:
        values = list(values)
        low = lane // (width * step) % 2
        low = (low if values[0].dtype == jnp.float32 else low.astype(jnp.float32).astype(values[0].dtype)) == 0
        for q in range(len(values)):
            if q // step % 2 == 0:
                a, b = values[q], values[q + step]
                values[q] = jnp.where(low, a, pltpu.roll(b, width * step, b.ndim - 1))
                values[q + step] = jnp.where(low, pltpu.roll(a, LANES - width * step, a.ndim - 1), b)
        step //= 2
    return values


def prepare_kernel(
    ids,
    library,
    mask,
    group,
    following,
    shifts,
    coef,
    after,
    edges,
    picked,
    wide,
    rows,
    made,
    gains,
    own_tail,
    tail,
    edge,
    row_sem,
    in_sem,
    tail_sem,
    out_sem,
    gain_sem,
    after_sem,
    edge_sem,
):
    stations = library.shape[1]
    total = mask.shape[1]
    position = lax.axis_index("tm")
    for k in range(SLOTS):
        pltpu.make_async_copy(library.at[ids[k // KB, k % KB]], picked.at[k], in_sem).start()
    for k in range(SLOTS):
        pltpu.make_async_copy(mask.at[pl.ds(ids[k // KB, k % KB], 1)], rows.at[pl.ds(k, 1)], row_sem).start()
    tail_in = pltpu.make_async_copy(following.at[pl.ds(position * stations, stations)], own_tail, tail_sem)
    tail_in.start()

    for k in range(SLOTS):
        pltpu.make_async_copy(library.at[0], picked.at[k], in_sem).wait()
    for k in range(SLOTS):
        wide[k] = picked[k].astype(jnp.float32)
    tail_in.wait()
    tail[...] = jnp.concatenate([own_tail[...], jnp.zeros((stations, 1), jnp.bfloat16)], axis=1)
    tail_out = pltpu.make_async_copy(tail, after, after_sem)
    tail_out.start()

    lane = lane_ids((PH, LANES))
    row = lax.broadcasted_iota(jnp.int32, (PH, LANES), 0)

    def part(c, carry):
        rest = [jnp.zeros((PH, LANES), jnp.float32) for _ in range(SLOTS)]
        for i in range(TURNS):
            s = c * TURNS + i
            inside = lane >= row + PH * i
            wrapped = lane < PH * i
            halves = []
            for k in range(SLOTS):
                template = wide[k, pl.ds(s, 1), :]
                turned = [
                    pltpu.roll(
                        jnp.broadcast_to(template[:, h * LANES : (h + 1) * LANES], (PH, LANES)),
                        PH * i,
                        1,
                        stride=1,
                        stride_axis=0,
                    )
                    for h in range(W // LANES)
                ]
                ahead = jnp.where(wrapped, turned[-1], 0.0)
                rest[k] = jnp.where(inside, rest[k], jnp.where(wrapped, rest[k], turned[-1]))
                columns = [jnp.where(inside, turned[h], turned[h - 1] if h else ahead) for h in range(W // LANES)]
                halves.append(jnp.concatenate(columns, axis=1))
            for pair in range(SLOTS // 2):
                value = jnp.concatenate(halves[2 * pair : 2 * pair + 2], axis=0).astype(jnp.bfloat16)
                made[s, 2 * PH * pair : 2 * PH * (pair + 1), :] = value
        edge[c] = jnp.concatenate(rest, axis=0).astype(jnp.bfloat16)
        span = pl.ds(c * TURNS, TURNS)
        pltpu.make_async_copy(made.at[span], shifts.at[span], out_sem).start()
        return carry

    lax.fori_loop(0, stations // TURNS, part, 0)
    edge_out = pltpu.make_async_copy(edge, edges, edge_sem)
    edge_out.start()

    members = lax.broadcasted_iota(jnp.int32, (G, total), 0) == group[...]
    members = members.astype(jnp.float32).astype(jnp.bfloat16)
    pltpu.make_async_copy(mask.at[pl.ds(0, SLOTS)], rows, row_sem).wait()
    counts = lax.dot_general(
        rows[...].astype(jnp.float32).astype(jnp.bfloat16),
        members,
        (((1,), (1,)), ((), ())),
        preferred_element_type=jnp.float32,
    )
    first = lax.axis_index("sta") * (stations * lax.axis_size("tm")) + position * stations
    block = pl.multiple_of(first // LANES * LANES, LANES)
    own_group = jnp.broadcast_to(group[:, pl.ds(block, LANES)], (G, LANES))
    own_mask = rows[:, pl.ds(block, LANES)].astype(jnp.float32)
    own = (lax.broadcasted_iota(jnp.int32, (G, LANES), 0) == own_group).astype(jnp.float32)
    per_station = jnp.dot(counts, own, preferred_element_type=jnp.float32, precision=lax.Precision.HIGHEST)
    scaled = own_mask / jnp.sqrt(jnp.float32(W * G) * jnp.maximum(per_station, 1.0))
    if stations % LANES:
        scaled = pltpu.roll(scaled, LANES - (first - block), 1)
    sums = jnp.zeros((stations, LANES), jnp.float32)
    for k in range(SLOTS):
        values = jnp.square(wide[k])
        values = sum(values[:, h * LANES : (h + 1) * LANES] for h in range(W // LANES))
        high = values.astype(jnp.bfloat16)
        low = (values - high.astype(jnp.float32)).astype(jnp.bfloat16)
        column = (lane_ids((LANES, LANES)) == k).astype(jnp.float32).astype(jnp.bfloat16)
        sums = sums + jnp.dot(high, column, preferred_element_type=jnp.float32)
        sums = sums + jnp.dot(low, column, preferred_element_type=jnp.float32)
    if stations < LANES:
        sums = jnp.concatenate([sums, jnp.zeros((LANES - stations, LANES), jnp.float32)], axis=0)
    gains[...] = scaled / jnp.sqrt(sums.T[:SLOTS] / W + epsilon)
    gains_out = pltpu.make_async_copy(gains, coef, gain_sem)
    gains_out.start()

    gains_out.wait()
    tail_out.wait()
    pltpu.make_async_copy(made, shifts, out_sem).wait()
    edge_out.wait()


def prepare(template_ids, library, channel_mask, station_group, following):
    stations = library.shape[1]
    total = channel_mask.shape[1]
    inputs = template_ids, library, channel_mask, station_group.reshape(1, total), following
    return pl.pallas_call(
        prepare_kernel,
        out_shape=(
            pltpu.HBM((stations, SLOTS * PH, W), jnp.bfloat16),
            pltpu.HBM((SLOTS, LANES), jnp.float32),
            pltpu.HBM((stations, W), jnp.bfloat16),
            pltpu.HBM((stations // TURNS, SLOTS * PH, LANES), jnp.bfloat16),
        ),
        in_specs=[
            pl.BlockSpec(memory_space=pltpu.SMEM),
            pl.BlockSpec(memory_space=pl.ANY),
            pl.BlockSpec(memory_space=pl.ANY),
            pl.BlockSpec(memory_space=pltpu.VMEM),
            pl.BlockSpec(memory_space=pl.ANY),
        ],
        out_specs=[pl.BlockSpec(memory_space=pl.ANY)] * 4,
        scratch_shapes=[
            pltpu.VMEM((SLOTS, stations, W), jnp.bfloat16),
            pltpu.VMEM((SLOTS, stations, W), jnp.float32),
            pltpu.VMEM((SLOTS, total), jnp.int32),
            pltpu.VMEM((stations, SLOTS * PH, W), jnp.bfloat16),
            pltpu.VMEM((SLOTS, LANES), jnp.float32),
            pltpu.VMEM((stations, following.shape[1]), jnp.bfloat16),
            pltpu.VMEM((stations, W), jnp.bfloat16),
            pltpu.VMEM((stations // TURNS, SLOTS * PH, LANES), jnp.bfloat16),
        ]
        + [pltpu.SemaphoreType.DMA] * 7,
        compiler_params=pltpu.CompilerParams(vmem_limit_bytes=VMEM),
        cost_estimate=pl.CostEstimate(flops=10_000_000, bytes_accessed=20_000_000, transcendentals=0),
        name="prepare",
    )(*(pltpu.with_memory_space_constraint(v, pltpu.HBM) for v in inputs))


def correlate_kernel(moved, following, shifts, coef, edges, out, held, gains, edge, tail, phases, inverse, windows, held_sems, gain_sem, edge_sem, tail_sem):
    owners, stations, block_len = moved.shape
    width = block_len // PH
    tiles = owners * block_len // (LANES * PH)
    per_tile = LANES // width

    tail_copy = pltpu.make_async_copy(following, tail, tail_sem)
    tail_copy.start()
    bounds = [0]
    for size in PARTS:
        bounds.append(min(stations, bounds[-1] + size))
    bounds[-1] = stations

    def held_copies(stage):
        for n, when in enumerate(START):
            if when == stage and bounds[n] < bounds[n + 1]:
                held_copy(n).start()

    def held_copy(n):
        span = pl.ds(bounds[n], bounds[n + 1] - bounds[n])
        return pltpu.make_async_copy(shifts.at[span], held.at[span], held_sems.at[n])

    gain_copy = pltpu.make_async_copy(coef, gains, gain_sem)
    gain_copy.start()
    edge_copy = pltpu.make_async_copy(edges, edge, edge_sem)
    held_copies(0)
    edge_copy.start()

    time = lax.broadcasted_iota(jnp.int32, (W, W), 0)
    place = lax.broadcasted_iota(jnp.int32, (W, W), 1)
    order = (time == place % TAPS * PH + place // TAPS).astype(jnp.float32).astype(jnp.bfloat16)

    def split(rows):
        value = jnp.dot(rows, order, preferred_element_type=jnp.float32).astype(jnp.bfloat16)
        return [value[:, h * LANES : (h + 1) * LANES] for h in range(W // LANES)]

    def keep(target, j, parts):
        parts = jnp.stack([v.astype(jnp.float32) for v in parts])
        target[j] = jnp.swapaxes(parts, 0, 1)

    here = (time >= place % TAPS * PH + place // TAPS).astype(jnp.float32).astype(jnp.bfloat16)
    beyond = (time < place % TAPS * PH + place // TAPS).astype(jnp.float32).astype(jnp.bfloat16)

    def squares(rows):
        value = jnp.square(rows.astype(jnp.float32))
        high = value.astype(jnp.bfloat16)
        return high, (value - high.astype(jnp.float32)).astype(jnp.bfloat16)

    each = W // block_len
    rows = [
        jnp.concatenate([moved[q * each + e] for e in range(each)], axis=1) for q in range(tiles * PIECES)
    ]
    for j in range(tiles):
        pieces = [split(r) for r in rows[j * PIECES : (j + 1) * PIECES]]
        keep(phases, j, [v for h in range(PH // PIECES) for v in swap_groups([p[h] for p in pieces], TAPS)])

    squared = [squares(r) for r in rows]
    for j in range(tiles):
        pieces = []
        for q in range(j * PIECES, (j + 1) * PIECES):
            terms = [(part, here) for part in squared[q]]
            if q + 1 < len(rows):
                terms += [(part, beyond) for part in squared[q + 1]]
            energy = sum(jnp.dot(part, matrix, preferred_element_type=jnp.float32) for part, matrix in terms)
            pieces.append([energy[:, h * LANES : (h + 1) * LANES] for h in range(W // LANES)])
        values = [v for h in range(PH // PIECES) for v in swap_groups([p[h] for p in pieces], TAPS)]
        if j < tiles - 1:
            values = [lax.rsqrt(v / W + epsilon) for v in values]
        keep(inverse, j, values)

    held_copies(1)
    tail_copy.wait()
    rows.append(tail[...])
    last = split(rows[-1])
    keep(
        phases,
        tiles,
        [
            pltpu.roll(last[p // PIECES], LANES - TAPS * (p % PIECES), 1) if p % PIECES else last[p // PIECES]
            for p in range(PH)
        ],
    )

    ahead = time - place % LANES - place // LANES
    for parity in range(2):
        for n in range(len(MADE) + 1):
            if n:
                matrix = ahead == 2 * MADE[n - 1] - parity
            else:
                matrix = jnp.logical_and(ahead == TAPS - parity, place // LANES == parity)
            matrix = matrix.astype(jnp.float32).astype(jnp.bfloat16)
            for j in range(tiles):
                value = jnp.concatenate([phases[j], phases[j + 1]], axis=2).reshape(stations // 2, 2, PH, W)[:, parity]
                value = value.reshape(stations // 2 * PH, W).astype(jnp.bfloat16)
                value = jnp.dot(value, matrix, preferred_element_type=jnp.float32)
                value = [value[:, h * LANES : (h + 1) * LANES].reshape(stations // 2, PH, LANES) for h in range(2)]
                windows[n, j, parity] = jnp.concatenate(value, axis=1).astype(jnp.bfloat16)

    extra = sum(jnp.dot(part, beyond, preferred_element_type=jnp.float32) for part in squares(rows[-1]))
    lane = lane_ids((stations, LANES))
    parts = []
    for p in range(PH):
        piece = extra[:, p // PIECES * LANES : (p // PIECES + 1) * LANES]
        if p % PIECES != PIECES - 1:
            piece = pltpu.roll(piece, TAPS * (PIECES - 1 - p % PIECES), 1)
        parts.append(jnp.where(lane >= LANES - TAPS, piece, 0.0))
    parts = jnp.swapaxes(jnp.stack(parts), 0, 1)
    inverse[tiles - 1] = lax.rsqrt((inverse[tiles - 1] + parts) / W + epsilon)

    nothing = jnp.zeros((2 * PH, LANES), jnp.bfloat16)

    def window(s, turn, j):
        own, after = phases[j, s], phases[j + 1, s]
        pairs = []
        for i in range(TAPS // 2):
            first = (2 * i - turn) % TAPS
            if (first + 1) // 2 in MADE:
                pairs.append(windows[1 + MADE.index((first + 1) // 2), j, turn % 2, s // 2])
            else:
                pair = [shifted(own, after, by % TAPS) for by in (first, first + 1)]
                pairs.append(jnp.concatenate(pair, axis=0).astype(jnp.bfloat16))
        return jnp.concatenate(pairs, axis=0)

    def two_stations(group, turn, totals):
        s = group * TURNS + turn
        results = []
        for j in range(tiles):
            ends = [
                jnp.concatenate([windows[0, j, e, s // 2] if i == turn // 2 else nothing for i in range(LANES // (2 * PH))], axis=0)
                for e in range(2)
            ]
            ends = jnp.dot(edge[group], jnp.concatenate(ends, axis=1), preferred_element_type=jnp.float32)
            total = totals[j]
            for e in range(2):
                corr = jnp.dot(held[s + e], window(s + e, turn + e, j), preferred_element_type=jnp.float32)
                corr = (corr + ends[:, e * LANES : (e + 1) * LANES]).reshape(SLOTS, PH, LANES)
                scale = inverse[j, s + e]
                total = tuple(total[k] + (corr[k] * scale) * gains[k, s + e] for k in range(SLOTS))
            results.append(total)
        return tuple(results)

    totals = tuple(tuple(jnp.zeros((PH, LANES), jnp.float32) for _ in range(SLOTS)) for _ in range(tiles))
    gain_copy.wait()
    edge_copy.wait()

    for n in range(len(PARTS)):
        if bounds[n] < bounds[n + 1]:
            if n == 0:
                held_copies(2)
            held_copy(n).wait()
            held_copies(3 + n)
            for s in range(bounds[n], bounds[n + 1], 2):
                totals = two_stations(s // TURNS, s % TURNS, totals)

    lane = lane_ids((KB, LANES))
    source = lane % PH * width + lane // PH
    for j in range(tiles):
        for b in range(NB):
            tile = jnp.swapaxes(jnp.stack(totals[j][b * KB : (b + 1) * KB]), 0, 1)
            for at, value in enumerate(swap_groups([tile[p] for p in range(PH)], width)):
                out[j * per_tile + at, b] = jnp.take_along_axis(value, source, axis=1)


def correlate(moved, following, shifts, coef, edges):
    owners, stations, block_len = moved.shape
    tiles = owners * block_len // (LANES * PH)
    return pl.pallas_call(
        correlate_kernel,
        out_shape=jax.ShapeDtypeStruct((owners, NB, KB, LANES), jnp.float32),
        in_specs=[
            pl.BlockSpec(memory_space=pltpu.VMEM),
            pl.BlockSpec(memory_space=pl.ANY),
            pl.BlockSpec(memory_space=pl.ANY),
            pl.BlockSpec(memory_space=pl.ANY),
            pl.BlockSpec(memory_space=pl.ANY),
        ],
        out_specs=pl.BlockSpec(memory_space=pltpu.VMEM),
        scratch_shapes=[
            pltpu.VMEM(shifts.shape, jnp.bfloat16),
            pltpu.SMEM(coef.shape, jnp.float32),
            pltpu.VMEM(edges.shape, jnp.bfloat16),
            pltpu.VMEM(following.shape, jnp.bfloat16),
            pltpu.VMEM((tiles + 1, stations, PH, LANES), jnp.float32),
            pltpu.VMEM((tiles, stations, PH, LANES), jnp.float32),
            pltpu.VMEM((len(MADE) + 1, tiles, 2, stations // 2, 2 * PH, LANES), jnp.bfloat16),
            pltpu.SemaphoreType.DMA((len(PARTS),)),
            pltpu.SemaphoreType.DMA,
            pltpu.SemaphoreType.DMA,
            pltpu.SemaphoreType.DMA,
        ],
        compiler_params=pltpu.CompilerParams(vmem_limit_bytes=VMEM),
        cost_estimate=pl.CostEstimate(flops=1_200_000_000, bytes_accessed=10_000_000, transcendentals=0),
        name="correlate",
    )(moved, *(pltpu.with_memory_space_constraint(v, pltpu.HBM) for v in (following, shifts, coef, edges)))


def shards(records, following, library, template_ids, channel_mask, station_group):
    owners = lax.axis_size("tm")
    block_len = records.shape[1]
    stations = library.shape[1]
    moved = lax.all_to_all(records.reshape(owners, stations, block_len), "tm", split_axis=0, concat_axis=0)
    shifts, coef, after, edges = prepare(template_ids, library, channel_mask, station_group, following)
    partial_sum = correlate(moved, after, shifts, coef, edges)
    parts = lax.all_to_all(
        partial_sum.reshape(owners * NB, KB, block_len), ("tm", "sta"), split_axis=0, concat_axis=0
    )
    return jnp.sum(parts, axis=0)[None]


def solution(mesh):
    placed = (
        P("sta", ("days", "tm")),
        P("sta", "days"),
        P(None, ("sta", "tm"), None),
        P(),
        P(),
        P(),
    )
    return jax.shard_map(
        shards,
        mesh=mesh,
        in_specs=placed,
        out_specs=P("sta", None, ("days", "tm")),
        check_vma=False,
    )
```

```python
import functools

import jax
import jax.numpy as jnp
from jax import lax
from jax.experimental import pallas as pl
from jax.experimental.pallas import tpu as pltpu
from jax.sharding import PartitionSpec as P

W = 256
NB = 2
KB = 8
G = 128
SLOTS = NB * KB
PH = 8
LANES = 128
TAPS = W // PH
PIECES = LANES // TAPS
VMEM = 24 << 20
PARTS = (56, 72)
START = (0, 1)
TURNS = LANES // PH
MADE = (8, 4)

epsilon = 1e-06


def lane_ids(shape):
    return lax.broadcasted_iota(jnp.int32, shape, len(shape) - 1)


def shifted(here, after, by):
    if by == 0:
        return here
    lane = lane_ids(here.shape)
    return pltpu.roll(jnp.where(lane < by, after, here), LANES - by, here.ndim - 1)


def swap_groups(values, width):
    lane = lane_ids(values[0].shape)
    step = len(values) // 2
    while step:
        values = list(values)
        low = lane // (width * step) % 2
        low = (low if values[0].dtype == jnp.float32 else low.astype(jnp.float32).astype(values[0].dtype)) == 0
        for q in range(len(values)):
            if q // step % 2 == 0:
                a, b = values[q], values[q + step]
                values[q] = jnp.where(low, a, pltpu.roll(b, width * step, b.ndim - 1))
                values[q + step] = jnp.where(low, pltpu.roll(a, LANES - width * step, a.ndim - 1), b)
        step //= 2
    return values


def prepare_kernel(
    ids,
    library,
    mask,
    group,
    following,
    shifts,
    coef,
    after,
    edges,
    picked,
    wide,
    rows,
    made,
    gains,
    own_tail,
    tail,
    edge,
    row_sem,
    in_sem,
    tail_sem,
    out_sem,
    gain_sem,
    after_sem,
    edge_sem,
):
    stations = library.shape[1]
    total = mask.shape[1]
    position = lax.axis_index("tm")
    for k in range(SLOTS):
        pltpu.make_async_copy(library.at[ids[k // KB, k % KB]], picked.at[k], in_sem).start()
    for k in range(SLOTS):
        pltpu.make_async_copy(mask.at[pl.ds(ids[k // KB, k % KB], 1)], rows.at[pl.ds(k, 1)], row_sem).start()
    tail_in = pltpu.make_async_copy(following.at[pl.ds(position * stations, stations)], own_tail, tail_sem)
    tail_in.start()

    for k in range(SLOTS):
        pltpu.make_async_copy(library.at[0], picked.at[k], in_sem).wait()
    for k in range(SLOTS):
        wide[k] = picked[k].astype(jnp.float32)
    tail_in.wait()
    tail[...] = jnp.concatenate([own_tail[...], jnp.zeros((stations, 1), jnp.bfloat16)], axis=1)
    tail_out = pltpu.make_async_copy(tail, after, after_sem)
    tail_out.start()

    lane = lane_ids((PH, LANES))
    row = lax.broadcasted_iota(jnp.int32, (PH, LANES), 0)

    def part(c, carry):
        rest = [jnp.zeros((PH, LANES), jnp.float32) for _ in range(SLOTS)]
        for i in range(TURNS):
            s = c * TURNS + i
            inside = lane >= row + PH * i
            wrapped = lane < PH * i
            halves = []
            for k in range(SLOTS):
                template = wide[k, pl.ds(s, 1), :]
                turned = [
                    pltpu.roll(
                        jnp.broadcast_to(template[:, h * LANES : (h + 1) * LANES], (PH, LANES)),
                        PH * i,
                        1,
                        stride=1,
                        stride_axis=0,
                    )
                    for h in range(W // LANES)
                ]
                ahead = jnp.where(wrapped, turned[-1], 0.0)
                rest[k] = jnp.where(inside, rest[k], jnp.where(wrapped, rest[k], turned[-1]))
                columns = [jnp.where(inside, turned[h], turned[h - 1] if h else ahead) for h in range(W // LANES)]
                halves.append(jnp.concatenate(columns, axis=1))
            for pair in range(SLOTS // 2):
                value = jnp.concatenate(halves[2 * pair : 2 * pair + 2], axis=0).astype(jnp.bfloat16)
                made[s, 2 * PH * pair : 2 * PH * (pair + 1), :] = value
        edge[c] = jnp.concatenate(rest, axis=0).astype(jnp.bfloat16)
        span = pl.ds(c * TURNS, TURNS)
        pltpu.make_async_copy(made.at[span], shifts.at[span], out_sem).start()
        return carry

    lax.fori_loop(0, stations // TURNS, part, 0)
    edge_out = pltpu.make_async_copy(edge, edges, edge_sem)
    edge_out.start()

    members = lax.broadcasted_iota(jnp.int32, (G, total), 0) == group[...]
    members = members.astype(jnp.float32).astype(jnp.bfloat16)
    pltpu.make_async_copy(mask.at[pl.ds(0, SLOTS)], rows, row_sem).wait()
    counts = lax.dot_general(
        rows[...].astype(jnp.float32).astype(jnp.bfloat16),
        members,
        (((1,), (1,)), ((), ())),
        preferred_element_type=jnp.float32,
    )
    first = lax.axis_index("sta") * (stations * lax.axis_size("tm")) + position * stations
    block = pl.multiple_of(first // LANES * LANES, LANES)
    own_group = jnp.broadcast_to(group[:, pl.ds(block, LANES)], (G, LANES))
    own_mask = rows[:, pl.ds(block, LANES)].astype(jnp.float32)
    own = (lax.broadcasted_iota(jnp.int32, (G, LANES), 0) == own_group).astype(jnp.float32)
    per_station = jnp.dot(counts, own, preferred_element_type=jnp.float32, precision=lax.Precision.HIGHEST)
    scaled = own_mask / jnp.sqrt(jnp.float32(W * G) * jnp.maximum(per_station, 1.0))
    if stations % LANES:
        scaled = pltpu.roll(scaled, LANES - (first - block), 1)
    sums = jnp.zeros((stations, LANES), jnp.float32)
    for k in range(SLOTS):
        values = jnp.square(wide[k])
        values = sum(values[:, h * LANES : (h + 1) * LANES] for h in range(W // LANES))
        high = values.astype(jnp.bfloat16)
        low = (values - high.astype(jnp.float32)).astype(jnp.bfloat16)
        column = (lane_ids((LANES, LANES)) == k).astype(jnp.float32).astype(jnp.bfloat16)
        sums = sums + jnp.dot(high, column, preferred_element_type=jnp.float32)
        sums = sums + jnp.dot(low, column, preferred_element_type=jnp.float32)
    if stations < LANES:
        sums = jnp.concatenate([sums, jnp.zeros((LANES - stations, LANES), jnp.float32)], axis=0)
    gains[...] = scaled / jnp.sqrt(sums.T[:SLOTS] / W + epsilon)
    gains_out = pltpu.make_async_copy(gains, coef, gain_sem)
    gains_out.start()

    gains_out.wait()
    tail_out.wait()
    pltpu.make_async_copy(made, shifts, out_sem).wait()
    edge_out.wait()


def prepare(template_ids, library, channel_mask, station_group, following):
    stations = library.shape[1]
    total = channel_mask.shape[1]
    inputs = template_ids, library, channel_mask, station_group.reshape(1, total), following
    return pl.pallas_call(
        prepare_kernel,
        out_shape=(
            pltpu.HBM((stations, SLOTS * PH, W), jnp.bfloat16),
            pltpu.HBM((SLOTS, LANES), jnp.float32),
            pltpu.HBM((stations, W), jnp.bfloat16),
            pltpu.HBM((stations // TURNS, SLOTS * PH, LANES), jnp.bfloat16),
        ),
        in_specs=[
            pl.BlockSpec(memory_space=pltpu.SMEM),
            pl.BlockSpec(memory_space=pl.ANY),
            pl.BlockSpec(memory_space=pl.ANY),
            pl.BlockSpec(memory_space=pltpu.VMEM),
            pl.BlockSpec(memory_space=pl.ANY),
        ],
        out_specs=[pl.BlockSpec(memory_space=pl.ANY)] * 4,
        scratch_shapes=[
            pltpu.VMEM((SLOTS, stations, W), jnp.bfloat16),
            pltpu.VMEM((SLOTS, stations, W), jnp.float32),
            pltpu.VMEM((SLOTS, total), jnp.int32),
            pltpu.VMEM((stations, SLOTS * PH, W), jnp.bfloat16),
            pltpu.VMEM((SLOTS, LANES), jnp.float32),
            pltpu.VMEM((stations, following.shape[1]), jnp.bfloat16),
            pltpu.VMEM((stations, W), jnp.bfloat16),
            pltpu.VMEM((stations // TURNS, SLOTS * PH, LANES), jnp.bfloat16),
        ]
        + [pltpu.SemaphoreType.DMA] * 7,
        compiler_params=pltpu.CompilerParams(vmem_limit_bytes=VMEM),
        cost_estimate=pl.CostEstimate(flops=10_000_000, bytes_accessed=20_000_000, transcendentals=0),
        name="prepare",
    )(*(pltpu.with_memory_space_constraint(v, pltpu.HBM) for v in inputs))


def correlate_kernel(moved, following, shifts, coef, edges, out, held, gains, edge, tail, phases, inverse, windows, held_sems, gain_sem, edge_sem, tail_sem):
    owners, stations, block_len = moved.shape
    width = block_len // PH
    tiles = owners * block_len // (LANES * PH)
    per_tile = LANES // width

    tail_copy = pltpu.make_async_copy(following, tail, tail_sem)
    tail_copy.start()
    bounds = [0]
    for size in PARTS:
        bounds.append(min(stations, bounds[-1] + size))
    bounds[-1] = stations

    def held_copies(stage):
        for n, when in enumerate(START):
            if when == stage and bounds[n] < bounds[n + 1]:
                held_copy(n).start()

    def held_copy(n):
        span = pl.ds(bounds[n], bounds[n + 1] - bounds[n])
        return pltpu.make_async_copy(shifts.at[span], held.at[span], held_sems.at[n])

    gain_copy = pltpu.make_async_copy(coef, gains, gain_sem)
    gain_copy.start()
    edge_copy = pltpu.make_async_copy(edges, edge, edge_sem)
    edge_copy.start()
    held_copies(0)

    time = lax.broadcasted_iota(jnp.int32, (W, W), 0)
    place = lax.broadcasted_iota(jnp.int32, (W, W), 1)
    order = (time == place % TAPS * PH + place // TAPS).astype(jnp.float32).astype(jnp.bfloat16)

    def split(rows):
        value = jnp.dot(rows, order, preferred_element_type=jnp.float32).astype(jnp.bfloat16)
        return [value[:, h * LANES : (h + 1) * LANES] for h in range(W // LANES)]

    def keep(target, j, parts):
        parts = jnp.stack([v.astype(jnp.float32) for v in parts])
        target[j] = jnp.swapaxes(parts, 0, 1)

    here = (time >= place % TAPS * PH + place // TAPS).astype(jnp.float32).astype(jnp.bfloat16)
    beyond = (time < place % TAPS * PH + place // TAPS).astype(jnp.float32).astype(jnp.bfloat16)

    def squares(rows):
        value = jnp.square(rows.astype(jnp.float32))
        high = value.astype(jnp.bfloat16)
        return high, (value - high.astype(jnp.float32)).astype(jnp.bfloat16)

    each = W // block_len
    rows = [
        jnp.concatenate([moved[q * each + e] for e in range(each)], axis=1) for q in range(tiles * PIECES)
    ]
    for j in range(tiles):
        pieces = [split(r) for r in rows[j * PIECES : (j + 1) * PIECES]]
        keep(phases, j, [v for h in range(PH // PIECES) for v in swap_groups([p[h] for p in pieces], TAPS)])
    tail_copy.wait()
    rows.append(tail[...])
    last = split(rows[-1])
    keep(
        phases,
        tiles,
        [
            pltpu.roll(last[p // PIECES], LANES - TAPS * (p % PIECES), 1) if p % PIECES else last[p // PIECES]
            for p in range(PH)
        ],
    )

    held_copies(1)

    ahead = time - place % LANES - place // LANES
    for parity in range(2):
        for n in range(len(MADE) + 1):
            if n:
                matrix = ahead == 2 * MADE[n - 1] - parity
            else:
                matrix = jnp.logical_and(ahead == TAPS - parity, place // LANES == parity)
            matrix = matrix.astype(jnp.float32).astype(jnp.bfloat16)
            for j in range(tiles):
                value = jnp.concatenate([phases[j], phases[j + 1]], axis=2).reshape(stations // 2, 2, PH, W)[:, parity]
                value = value.reshape(stations // 2 * PH, W).astype(jnp.bfloat16)
                value = jnp.dot(value, matrix, preferred_element_type=jnp.float32)
                value = [value[:, h * LANES : (h + 1) * LANES].reshape(stations // 2, PH, LANES) for h in range(2)]
                windows[n, j, parity] = jnp.concatenate(value, axis=1).astype(jnp.bfloat16)

    squared = [squares(r) for r in rows]
    for j in range(tiles):
        pieces = []
        for q in range(j * PIECES, (j + 1) * PIECES):
            energy = sum(
                jnp.dot(part, matrix, preferred_element_type=jnp.float32)
                for parts, matrix in ((squared[q], here), (squared[q + 1], beyond))
                for part in parts
            )
            energy = lax.rsqrt(energy / W + epsilon)
            pieces.append([energy[:, h * LANES : (h + 1) * LANES] for h in range(W // LANES)])
        keep(inverse, j, [v for h in range(PH // PIECES) for v in swap_groups([p[h] for p in pieces], TAPS)])

    nothing = jnp.zeros((2 * PH, LANES), jnp.bfloat16)

    def window(s, turn, j):
        own, after = phases[j, s], phases[j + 1, s]
        pairs = []
        for i in range(TAPS // 2):
            first = (2 * i - turn) % TAPS
            if (first + 1) // 2 in MADE:
                pairs.append(windows[1 + MADE.index((first + 1) // 2), j, turn % 2, s // 2])
            else:
                pair = [shifted(own, after, by % TAPS) for by in (first, first + 1)]
                pairs.append(jnp.concatenate(pair, axis=0).astype(jnp.bfloat16))
        return jnp.concatenate(pairs, axis=0)

    def two_stations(group, turn, totals):
        s = group * TURNS + turn
        results = []
        for j in range(tiles):
            ends = [
                jnp.concatenate([windows[0, j, e, s // 2] if i == turn // 2 else nothing for i in range(LANES // (2 * PH))], axis=0)
                for e in range(2)
            ]
            ends = jnp.dot(edge[group], jnp.concatenate(ends, axis=1), preferred_element_type=jnp.float32)
            total = totals[j]
            for e in range(2):
                corr = jnp.dot(held[s + e], window(s + e, turn + e, j), preferred_element_type=jnp.float32)
                corr = (corr + ends[:, e * LANES : (e + 1) * LANES]).reshape(SLOTS, PH, LANES)
                scale = inverse[j, s + e]
                total = tuple(total[k] + (corr[k] * scale) * gains[k, s + e] for k in range(SLOTS))
            results.append(total)
        return tuple(results)

    totals = tuple(tuple(jnp.zeros((PH, LANES), jnp.float32) for _ in range(SLOTS)) for _ in range(tiles))
    gain_copy.wait()
    edge_copy.wait()

    for n in range(len(PARTS)):
        if bounds[n] < bounds[n + 1]:
            if n == 0:
                held_copies(2)
            held_copy(n).wait()
            held_copies(3 + n)
            for s in range(bounds[n], bounds[n + 1], 2):
                totals = two_stations(s // TURNS, s % TURNS, totals)

    lane = lane_ids((KB, LANES))
    source = lane % PH * width + lane // PH
    for j in range(tiles):
        for b in range(NB):
            tile = jnp.swapaxes(jnp.stack(totals[j][b * KB : (b + 1) * KB]), 0, 1)
            for at, value in enumerate(swap_groups([tile[p] for p in range(PH)], width)):
                out[j * per_tile + at, b] = jnp.take_along_axis(value, source, axis=1)


def correlate(moved, following, shifts, coef, edges):
    owners, stations, block_len = moved.shape
    tiles = owners * block_len // (LANES * PH)
    return pl.pallas_call(
        correlate_kernel,
        out_shape=jax.ShapeDtypeStruct((owners, NB, KB, LANES), jnp.float32),
        in_specs=[
            pl.BlockSpec(memory_space=pltpu.VMEM),
            pl.BlockSpec(memory_space=pl.ANY),
            pl.BlockSpec(memory_space=pl.ANY),
            pl.BlockSpec(memory_space=pl.ANY),
            pl.BlockSpec(memory_space=pl.ANY),
        ],
        out_specs=pl.BlockSpec(memory_space=pltpu.VMEM),
        scratch_shapes=[
            pltpu.VMEM(shifts.shape, jnp.bfloat16),
            pltpu.SMEM(coef.shape, jnp.float32),
            pltpu.VMEM(edges.shape, jnp.bfloat16),
            pltpu.VMEM(following.shape, jnp.bfloat16),
            pltpu.VMEM((tiles + 1, stations, PH, LANES), jnp.float32),
            pltpu.VMEM((tiles, stations, PH, LANES), jnp.float32),
            pltpu.VMEM((len(MADE) + 1, tiles, 2, stations // 2, 2 * PH, LANES), jnp.bfloat16),
            pltpu.SemaphoreType.DMA((len(PARTS),)),
            pltpu.SemaphoreType.DMA,
            pltpu.SemaphoreType.DMA,
            pltpu.SemaphoreType.DMA,
        ],
        compiler_params=pltpu.CompilerParams(vmem_limit_bytes=VMEM),
        cost_estimate=pl.CostEstimate(flops=1_200_000_000, bytes_accessed=10_000_000, transcendentals=0),
        name="correlate",
    )(moved, *(pltpu.with_memory_space_constraint(v, pltpu.HBM) for v in (following, shifts, coef, edges)))


def shards(records, following, library, template_ids, channel_mask, station_group):
    owners = lax.axis_size("tm")
    block_len = records.shape[1]
    stations = library.shape[1]
    moved = lax.all_to_all(records.reshape(owners, stations, block_len), "tm", split_axis=0, concat_axis=0)
    shifts, coef, after, edges = prepare(template_ids, library, channel_mask, station_group, following)
    partial_sum = correlate(moved, after, shifts, coef, edges)
    parts = lax.all_to_all(
        partial_sum.reshape(owners * NB, KB, block_len), ("tm", "sta"), split_axis=0, concat_axis=0
    )
    return jnp.sum(parts, axis=0)[None]


def solution(mesh):
    placed = (
        P("sta", ("days", "tm")),
        P("sta", "days"),
        P(None, ("sta", "tm"), None),
        P(),
        P(),
        P(),
    )
    return jax.shard_map(
        shards,
        mesh=mesh,
        in_specs=placed,
        out_specs=P("sta", None, ("days", "tm")),
        check_vma=False,
    )
```
